256 devices in a mesh: seq: 32 (over x, z), tp: 8 (over y, core).
Axes of the slice: x: 4, y: 4, z: 8, core: 2. Of those that a mesh axis runs over, the one named last changes fastest.
Arguments:
- queries: bfloat16 [4096, 8192], P('seq', 'tp'), may hold values from -100 to 100, as said below
- key_rows: bfloat16 [4096, 1024], P('seq', 'tp'), may hold values from -4 to 4
- value_rows: bfloat16 [4096, 1024], P('seq', 'tp'), may hold values from -100 to 100
- text_mask: int32 [4096], P('seq'), may hold values from 0 to 1, as said below
- kept_slot: int32 [4096], P('seq'), may hold values from -1 to 1023, as said below
- norm_gain: float32 [8192], P('tp'), may hold values from 0.5 to 1.5
Outputs:
- context: bfloat16 [4096, 8192], P('seq', 'tp')
- visual_mass: float32 [4096], P('seq')
- kept_rows: bfloat16 [1024, 8192], P('seq', 'tp')
The draws below stay inside these ranges and needn't reach their ends.
Inputs may be any that keep to these rules, and one draw needn't show every extreme that they name: `queries`: queries of one token and head stay within the stated range. `text_mask`: the text tokens form two runs of one or more tokens: one that starts at token 0 and one that ends at the last token; together they hold one seventeenth of 4096, rounded down. All other tokens are visual. `kept_slot`: every slot 0 to 1023 is held by exactly one token; slot // 32 is the destination shard, so each destination receives exactly 32 tokens. At most 2 tokens of one shard of 128 tokens go to one destination, and some pair of shards reaches 2 in every draw. Within a destination, slots follow the order of the source shards. Other tokens hold -1.
All inputs are finite; a program needn't handle non-finite values.
Results may differ from the reference program's by a relative error of at most 0.0095.
Values may be sent and summed in bfloat16 or wider, within the bound.
No kernel may reach another device: no remote copies, remote signals or barrier semaphores. Data moves between devices by JAX's collectives and lax.ppermute only.
A program may use at most 64 MiB of HBM per device.

```python
import math
import jax
import jax.numpy as jnp
from jax import lax

H = 64
KVH = 8
HD = 128
TOK_DEV = 128
D = 8192
TOKENS = 4096
KEEP_DEV = 32
KEPT = 1024
CAP = 2
N_SEQ = 32


def shared_keys(key):
    return jnp.clip(jax.random.normal(key, (TOKENS, KVH, HD), jnp.float32), -4.0, 4.0)


def draw_key_rows(key, part):
    shared = shared_keys(key)
    return shared.reshape(TOKENS, KVH * HD).astype(jnp.bfloat16)


def draw_queries(key, part):
    key = jax.random.fold_in(key, 2)
    fresh = jnp.clip(jax.random.normal(key, (TOKENS, H, HD), jnp.float32), -6.0, 6.0)
    return fresh.reshape(TOKENS, H * HD).astype(jnp.bfloat16)


def draw_value_rows(key, part):
    key = jax.random.fold_in(key, 3)
    first, second, third = jax.random.split(key, 3)
    base = jnp.clip(jax.random.normal(first, (TOKENS, KVH, HD), jnp.float32), -6.0, 6.0)
    row_scale = jnp.exp(jax.random.uniform(second, (TOKENS, 1, 1), jnp.float32, math.log(0.3), math.log(3.0)))
    column_scale = jnp.exp(jax.random.uniform(third, (1, KVH, HD), jnp.float32, math.log(0.3), math.log(3.0)))
    head_scale = (3.0 ** (jnp.arange(KVH, dtype=jnp.float32) / max(KVH - 1, 1)) / 1.7)[None, :, None]
    result = jnp.clip(base * row_scale * column_scale * head_scale, -100.0, 100.0)
    return result.reshape(TOKENS, KVH * HD).astype(jnp.bfloat16)


def draw_text_mask(key, part):
    key = jax.random.fold_in(key, 5)
    text_total = TOKENS // 17
    lowest = max(1, text_total // 4)
    highest = max(lowest + 1, text_total // 2 + 1)
    prefix = jax.random.randint(key, (), lowest, highest, jnp.int32)
    positions = jnp.arange(TOKENS, dtype=jnp.int32)
    text = (positions < prefix) | (positions >= TOKENS - (text_total - prefix))
    return text.astype(jnp.int32)


def draw_kept_slot(key, part):
    key = jax.random.fold_in(key, 11)
    first, second, third = jax.random.split(key, 3)
    shards = N_SEQ
    half = shards // 2
    order = jax.random.permutation(first, shards)
    place_of = jnp.argsort(order)
    busy = place_of < half
    slot_pos = place_of % half
    shuffle = jax.random.permutation(second, shards) % half
    heavy = 3 * KEEP_DEV // 4
    light = KEEP_DEV - heavy
    spots = (slot_pos[:, None] + shuffle[None, :]) % half
    quota = jnp.where(busy[:, None], heavy, light)
    counts = jnp.clip(quota - CAP * spots, 0, CAP).astype(jnp.int32)
    before_src = jnp.cumsum(counts, axis=0) - counts
    upto = jnp.cumsum(counts, axis=1)
    begins = upto - counts
    kept_count = upto[:, -1]
    positions = jnp.arange(TOK_DEV, dtype=jnp.int32)
    dest_of = jnp.sum((positions[None, :, None] >= upto[:, None, :]).astype(jnp.int32), axis=2)
    dest_clip = jnp.minimum(dest_of, shards - 1)
    ranks = positions[None, :] - jnp.take_along_axis(begins, dest_clip, axis=1)
    offsets = jnp.take_along_axis(before_src, dest_clip, axis=1)
    valued = jnp.where(positions[None, :] < kept_count[:, None], dest_clip * KEEP_DEV + offsets + ranks, -1)
    shuffles = jax.vmap(lambda subkey: jax.random.permutation(subkey, TOK_DEV))(jax.random.split(third, shards))
    slots = jnp.zeros((shards, TOK_DEV), jnp.int32).at[jnp.arange(shards)[:, None], shuffles].set(valued.astype(jnp.int32))
    return slots.reshape(TOKENS)


def setup_inputs(seed: int = 0) -> dict:
    seeds = jax.random.split(jax.random.key(seed), 7)
    return {
        "queries": draw_queries(jax.random.fold_in(seeds[6], 71), 0),
        "key_rows": draw_key_rows(jax.random.fold_in(seeds[6], 71), 0),
        "value_rows": draw_value_rows(jax.random.fold_in(seeds[6], 71), 0),
        "text_mask": draw_text_mask(jax.random.fold_in(seeds[6], 71), 0),
        "kept_slot": draw_kept_slot(jax.random.fold_in(seeds[6], 71), 0),
        "norm_gain": jnp.clip(1.0 + 0.1 * jax.random.normal(seeds[5], (D,), jnp.float32), 0.5, 1.5),
    }


def reference(queries, key_rows, value_rows, text_mask, kept_slot, norm_gain):
    count = queries.shape[0]
    group = H // KVH
    scale = 1.0 / math.sqrt(HD)
    positions = jnp.arange(count, dtype=jnp.int32)
    allowed = positions[None, :] <= positions[:, None]
    is_text = text_mask.astype(jnp.float32)
    query_heads = queries.reshape(count, H, HD)
    key_heads = key_rows.reshape(count, KVH, HD)
    value_heads = value_rows.reshape(count, KVH, HD)

    def one_head(head):
        shared = head // group
        query_one = query_heads[:, head, :]
        key_one = key_heads[:, shared, :]
        value_one = value_heads[:, shared, :]
        scores = jnp.dot(query_one, key_one.T, preferred_element_type=jnp.float32) * scale
        scores = jnp.where(allowed, scores, jnp.float32(-1e+30))
        row_max = lax.optimization_barrier(jnp.max(scores, axis=1))
        weights = jnp.where(allowed, jnp.exp(scores - row_max[:, None]), jnp.float32(0.0))
        row_total = lax.optimization_barrier(jnp.sum(weights, axis=1))
        mixed = jnp.dot(weights.astype(jnp.bfloat16), value_one, preferred_element_type=jnp.float32)
        mixed = mixed / row_total[:, None]
        probability = weights / row_total[:, None]
        column_mass = lax.optimization_barrier(jnp.sum(probability * is_text[:, None], axis=0))
        return (mixed, column_mass)
    mixed_all, mass_all = lax.map(one_head, jnp.arange(H, dtype=jnp.int32))
    context = jnp.transpose(mixed_all, (1, 0, 2)).reshape(count, H * HD).astype(jnp.bfloat16)
    visual_mass = lax.optimization_barrier(jnp.sum(mass_all, axis=0)) * (1.0 - is_text)
    wide = context.astype(jnp.float32)
    mean_square = lax.optimization_barrier(jnp.sum(wide * wide, axis=1)) / (H * HD)
    normed = (wide * lax.rsqrt(mean_square + 1e-06)[:, None] * norm_gain[None, :]).astype(jnp.bfloat16)
    target = jnp.where(kept_slot >= 0, kept_slot, KEPT).astype(jnp.int32)
    kept_rows = jnp.zeros((KEPT, H * HD), jnp.bfloat16).at[target].set(normed, mode='drop')
    return (context, visual_mass, kept_rows)
```

```python
import math

import jax
import jax.numpy as jnp
from jax import lax
from jax.experimental import pallas as pl
from jax.experimental.pallas import tpu as pltpu
from jax.sharding import Mesh, PartitionSpec as P

HD = 128
D = 8192
TOK = 128
GROUP = 8
ROWS = GROUP * TOK
NX = 4
NZ = 8
SHARDS = NX * NZ
KEEP = 32
SUB = 24
SEND = SHARDS * SUB
PICK = ROWS + 2 * TOK
PAY = 8 + KEEP
BLOCK = 256
SLAB = NZ * TOK
FACTOR = math.log2(math.e) / math.sqrt(HD)
LOW = -1e30
NT = (((1,), (1,)), ((), ()))
TN = (((0,), (0,)), ((), ()))
VMEM_BYTES = 48 * 1024 * 1024


def smem():
    return pl.BlockSpec(memory_space=pltpu.SMEM)


def vmem():
    return pl.BlockSpec(memory_space=pltpu.VMEM)


def params():
    return pltpu.CompilerParams(vmem_limit_bytes=VMEM_BYTES)


def rows_of_queries(q_ref, block):
    heads = BLOCK // TOK
    return jnp.concatenate(
        [q_ref[:, (block * heads + i) * HD : (block * heads + i + 1) * HD] for i in range(heads)],
        axis=0,
    )


def own_mask(z, width):
    token = lax.broadcasted_iota(jnp.int32, (BLOCK, width), 0) & (TOK - 1)
    key = lax.broadcasted_iota(jnp.int32, (BLOCK, width), 1)
    return key <= token + z * TOK


def flash(query, key, value, old, mask=None):
    scores = lax.dot_general(query, key, NT, preferred_element_type=jnp.float32)
    if mask is not None:
        scores = jnp.where(mask, scores, LOW)
    top = jnp.max(scores, axis=1, keepdims=True)
    if old is not None:
        top = jnp.maximum(old[0], top)
    weights = jnp.exp2((scores - top) * FACTOR)
    total = jnp.sum(weights, axis=1, keepdims=True)
    mixed = jnp.dot(weights.astype(jnp.bfloat16), value, preferred_element_type=jnp.float32)
    if old is not None:
        shrink = jnp.exp2((old[0] - top) * FACTOR)
        total = total + old[1] * shrink
        mixed = mixed + old[2] * shrink
    return top, total, mixed


def wide(column):
    return jnp.broadcast_to(column, (column.shape[0], 128))


def keys_of(ref):
    return ref[:, 0].reshape(-1, HD)


def values_of(ref):
    return ref[:, 1].reshape(-1, HD)


def own_kernel(place_ref, q_ref, slab_ref, slot_row_ref, top_ref, total_ref, mixed_ref, pick_ref):
    z = place_ref[1]
    key = keys_of(slab_ref)
    value = values_of(slab_ref)
    mask = own_mask(z, SLAB)
    for block in range(ROWS // BLOCK):
        rows = slice(block * BLOCK, (block + 1) * BLOCK)
        top, total, mixed = flash(rows_of_queries(q_ref, block), key, value, None, mask)
        top_ref[rows] = wide(top)
        total_ref[rows] = wide(total)
        mixed_ref[rows] = mixed
    slot_row = slot_row_ref[...]
    target_row = jnp.where(slot_row >= 0, slot_row >> 5, -1)
    target_col = jnp.transpose(jnp.broadcast_to(target_row, (TOK, TOK)))
    first = lax.broadcasted_iota(jnp.int32, (TOK, TOK), 0)
    second = lax.broadcasted_iota(jnp.int32, (TOK, TOK), 1)
    earlier = jnp.where((target_col == target_row) & (first < second), 1, 0)
    rank = jnp.sum(earlier, axis=0, keepdims=True)
    placed = jnp.where(target_row >= 0, target_row * 2 + rank, -1)[None]
    shape = (SHARDS, SUB, TOK)
    to = lax.broadcasted_iota(jnp.int32, shape, 0)
    sub = lax.broadcasted_iota(jnp.int32, shape, 1)
    lane = lax.broadcasted_iota(jnp.int32, shape, 2)
    head = jnp.where(sub < 16, sub & 7, -1)
    same = placed == to * 2 + (sub >> 3)

    def put(at, hit):
        picked = jnp.where(hit, 1.0, 0.0).reshape(SEND, TOK)
        pick_ref[:, at : at + TOK] = picked.astype(jnp.bfloat16)

    for h in range(GROUP):
        put(h * TOK, same & (head == h))
    put(ROWS, (placed == to * 2 + (sub - 18)) & ((sub == 18) | (sub == 19)))
    put(ROWS + TOK, lane == jnp.where(sub == 16, to, jnp.where(sub == 17, to + SHARDS, -1)))


def next_kernel(
    place_ref, q_ref, left_ref, right_ref, top_in, total_in, mixed_in, top_ref, total_ref, mixed_ref
):
    x = place_ref[0]
    top_ref[...] = top_in[...]
    total_ref[...] = total_in[...]
    mixed_ref[...] = mixed_in[...]

    def add(slab_ref):
        key = keys_of(slab_ref)
        value = values_of(slab_ref)
        for block in range(ROWS // BLOCK):
            rows = slice(block * BLOCK, (block + 1) * BLOCK)
            old = (top_ref[rows, 0:1], total_ref[rows, 0:1], mixed_ref[rows])
            top, total, mixed = flash(rows_of_queries(q_ref, block), key, value, old)
            top_ref[rows] = wide(top)
            total_ref[rows] = wide(total)
            mixed_ref[rows] = mixed

    @pl.when(x > 0)
    def _():
        add(left_ref)

    @pl.when(x == NX - 1)
    def _():
        add(right_ref)


def last_kernel(
    place_ref,
    q_ref,
    far_left_ref,
    far_right_ref,
    own_ref,
    left_ref,
    right_ref,
    text_ref,
    slots_ref,
    pick_ref,
    top_in,
    total_in,
    mixed_in,
    context_ref,
    send_ref,
    top_ref,
    total_ref,
    mixed_ref,
    mass_ref,
):
    x = place_ref[0]
    z = place_ref[1]
    has_text = place_ref[2]
    top_ref[...] = top_in[...]
    total_ref[...] = total_in[...]
    mixed_ref[...] = mixed_in[...]
    mass_ref[...] = jnp.zeros_like(mass_ref)

    @pl.when(x >= 2)
    def _():
        key = jnp.concatenate([keys_of(far_left_ref), keys_of(far_right_ref)], axis=0)
        value = jnp.concatenate([values_of(far_left_ref), values_of(far_right_ref)], axis=0)
        for block in range(ROWS // BLOCK):
            rows = slice(block * BLOCK, (block + 1) * BLOCK)
            old = (top_ref[rows, 0:1], total_ref[rows, 0:1], mixed_ref[rows])
            top, total, mixed = flash(rows_of_queries(q_ref, block), key, value, old)
            top_ref[rows] = wide(top)
            total_ref[rows] = wide(total)
            mixed_ref[rows] = mixed

    context = (mixed_ref[...] / total_ref[...]).astype(jnp.bfloat16)
    for h in range(GROUP):
        context_ref[:, h * HD : (h + 1) * HD] = context[h * TOK : (h + 1) * TOK]

    @pl.when(has_text > 0)
    def _():
        text = jnp.concatenate([text_ref[...]] * (BLOCK // TOK), axis=0)[:, 0:1]
        mask = own_mask(z, SLAB)

        def mass_of(key, at, masked):
            shift = lax.rem(at, NX) * NZ
            added = jnp.zeros((1, SLAB), jnp.float32)
            for block in range(ROWS // BLOCK):
                rows = slice(block * BLOCK, (block + 1) * BLOCK)
                query = rows_of_queries(q_ref, block)
                scores = lax.dot_general(query, key, NT, preferred_element_type=jnp.float32)
                level = top_ref[rows, 0:1] * FACTOR + jnp.log2(total_ref[rows, 0:1])
                level = jnp.where(text > 0.0, level, -LOW)
                probability = jnp.exp2(scores * FACTOR - level)
                if masked:
                    probability = jnp.where(mask, probability, 0.0)
                added = added + jnp.sum(probability, axis=0, keepdims=True)
            for i in range(NZ):
                mass_ref[pl.ds(shift + i, 1), :] = added[:, i * TOK : (i + 1) * TOK]

        mass_of(keys_of(own_ref), x, True)

        @pl.when(x > 0)
        def _():
            mass_of(keys_of(left_ref), x + NX - 1, False)

        @pl.when(x == NX - 1)
        def _():
            mass_of(keys_of(right_ref), x + 1, False)

        @pl.when(x >= 2)
        def _():
            key = jnp.concatenate([keys_of(far_left_ref), keys_of(far_right_ref)], axis=0)
            mass_of(key, x + 2, False)

    mass = mass_ref[...]
    high = mass.astype(jnp.bfloat16).astype(jnp.float32)
    low = mass - high
    both = jnp.concatenate([high, low, jnp.zeros((TOK - 2 * SHARDS, HD), jnp.float32)], axis=0)
    slots = slots_ref[...]
    slots = jnp.where(slots >= 0, (slots & (KEEP - 1)) + 1, 0).astype(jnp.float32)
    source = jnp.concatenate(
        [context, slots.astype(jnp.bfloat16), both.astype(jnp.bfloat16)], axis=0
    )
    send_ref[...] = jnp.dot(pick_ref[...], source, preferred_element_type=jnp.float32).astype(
        jnp.bfloat16
    )


def place_kernel(got_ref, rows_ref, pay_ref):
    got = got_ref[...].astype(jnp.float32).reshape(SHARDS, SUB, HD)
    mass = jnp.sum(got[:, 16:17, :] + got[:, 17:18, :], axis=0)
    slots = jnp.concatenate(
        [
            jnp.broadcast_to(got[:, 18:19, :], (SHARDS, 8, HD)),
            jnp.broadcast_to(got[:, 19:20, :], (SHARDS, 8, HD)),
            jnp.zeros((SHARDS, 8, HD), jnp.float32),
        ],
        axis=1,
    ).astype(jnp.int32)
    shape = (SHARDS, SUB, HD)
    head = lax.broadcasted_iota(jnp.int32, shape, 1) & 7
    lane = lax.broadcasted_iota(jnp.int32, shape, 2)
    parts = []
    for half in range(2):
        hit = (slots == (lane & (KEEP - 1)) + 1) & (head == (lane >> 5) + 4 * half)
        parts.append(jnp.where(hit, 1.0, 0.0).reshape(SEND, HD))
    put = jnp.concatenate(parts, axis=1).astype(jnp.bfloat16)
    rows = lax.dot_general(put, got_ref[...], TN, preferred_element_type=jnp.float32)
    rows_ref[...] = rows
    squares = jnp.sum((rows * rows).reshape(GROUP, KEEP, HD), axis=0)
    squares = jnp.sum(squares, axis=1, keepdims=True)
    pay_ref[...] = jnp.concatenate([jnp.broadcast_to(mass, (8, HD)), wide(squares)], axis=0)


def finish_kernel(a_ref, b_ref, c_ref, d_ref, rows_ref, gain_ref, text_ref, mass_ref, kept_ref):
    pay = (a_ref[...] + b_ref[...]) + (c_ref[...] + d_ref[...])
    mass_ref[...] = pay[0:1] * (1.0 - text_ref[...].astype(jnp.float32))
    factor = lax.rsqrt(pay[8:] / D + 1e-06)
    for h in range(GROUP):
        columns = slice(h * HD, (h + 1) * HD)
        kept_ref[:, columns] = (
            rows_ref[h * KEEP : (h + 1) * KEEP] * factor * gain_ref[:, columns]
        ).astype(jnp.bfloat16)


def shape_of(shape, dtype):
    return jax.ShapeDtypeStruct(shape, dtype)


def shifted(value, axis, step, count):
    return lax.ppermute(value, axis, [(i, (i + step) % count) for i in range(count)])


def on_device(queries, key_rows, value_rows, text_mask, kept_slot, norm_gain):
    f32, bf16 = jnp.float32, jnp.bfloat16
    x = lax.axis_index("x")
    z = lax.axis_index("z")
    place = jnp.stack([x, z, jnp.max(text_mask)]).astype(jnp.int32)
    text_columns = jnp.broadcast_to(text_mask[:, None], (TOK, HD)).astype(f32)
    slot_columns = jnp.broadcast_to(kept_slot[:, None], (TOK, HD))

    both = jnp.stack([key_rows, value_rows])
    own = lax.all_to_all(
        jnp.broadcast_to(both[None], (NZ, 2, TOK, HD)), "z", split_axis=0, concat_axis=0, tiled=True
    )
    left = shifted(own, "x", 1, NX)
    right = shifted(own, "x", -1, NX)
    half = NZ // 2
    far_left = shifted(left[:half], "x", 1, NX)
    far_right = shifted(right[half:], "x", -1, NX)

    state = [shape_of((ROWS, HD), f32)] * 3
    pair = 4 * ROWS * SLAB * HD
    top, total, mixed, pick = pl.pallas_call(
        own_kernel,
        in_specs=[smem(), vmem(), vmem(), vmem()],
        out_specs=[vmem()] * 4,
        out_shape=state + [shape_of((SEND, PICK), bf16)],
        compiler_params=params(),
        cost_estimate=pl.CostEstimate(
            flops=pair, bytes_accessed=5 * 2**20, transcendentals=ROWS * SLAB
        ),
        name="own_slab",
    )(place, queries, own, kept_slot[None])
    top, total, mixed = pl.pallas_call(
        next_kernel,
        in_specs=[smem()] + [vmem()] * 6,
        out_specs=[vmem()] * 3,
        out_shape=state,
        compiler_params=params(),
        cost_estimate=pl.CostEstimate(
            flops=2 * pair, bytes_accessed=5 * 2**20, transcendentals=2 * ROWS * SLAB
        ),
        name="next_slabs",
    )(place, queries, left, right, top, total, mixed)
    context, send = pl.pallas_call(
        last_kernel,
        in_specs=[smem()] + [vmem()] * 12,
        out_specs=[vmem()] * 2,
        out_shape=[shape_of((TOK, GROUP * HD), bf16), shape_of((SEND, HD), bf16)],
        scratch_shapes=[pltpu.VMEM((ROWS, HD), f32)] * 3 + [pltpu.VMEM((SHARDS, HD), f32)],
        compiler_params=params(),
        cost_estimate=pl.CostEstimate(
            flops=3 * pair, bytes_accessed=6 * 2**20, transcendentals=5 * ROWS * SLAB
        ),
        name="last_slab",
    )(
        place, queries, far_left, far_right, own, left, right, text_columns, slot_columns, pick,
        top, total, mixed,
    )
    got = lax.all_to_all(
        send.reshape(SHARDS, SUB, HD), ("x", "z"), split_axis=0, concat_axis=0, tiled=True
    ).reshape(SEND, HD)
    rows, pay = pl.pallas_call(
        place_kernel,
        in_specs=[vmem()],
        out_specs=[vmem()] * 2,
        out_shape=[shape_of((GROUP * KEEP, HD), f32), shape_of((PAY, HD), f32)],
        compiler_params=params(),
        name="place_rows",
    )(got)
    pay = pay + shifted(pay, "core", 1, 2)
    pays = [pay] + [shifted(pay, "y", step, 4) for step in (1, 2, 3)]
    mass, kept = pl.pallas_call(
        finish_kernel,
        in_specs=[vmem()] * 7,
        out_specs=[vmem()] * 2,
        out_shape=[shape_of((1, TOK), f32), shape_of((KEEP, GROUP * HD), bf16)],
        compiler_params=params(),
        name="finish",
    )(*pays, rows, norm_gain[None], text_mask[None])
    return context, mass[0], kept


def solution(mesh):
    cut = Mesh(mesh.devices.reshape(NX, NZ, 4, 2), ("x", "z", "y", "core"))
    seq, tp = ("x", "z"), ("y", "core")
    placed = (P(seq, tp), P(seq, tp), P(seq, tp), P(seq), P(seq), P(tp))
    return jax.shard_map(
        on_device,
        mesh=cut,
        in_specs=placed,
        out_specs=(P(seq, tp), P(seq), P(seq, tp)),
        check_vma=False,
    )
```

```python
import math

import jax
import jax.numpy as jnp
from jax import lax
from jax.experimental import pallas as pl
from jax.experimental.pallas import tpu as pltpu
from jax.sharding import Mesh, PartitionSpec as P

HD = 128
D = 8192
TOK = 128
GROUP = 8
ROWS = GROUP * TOK
NX = 4
NZ = 8
SHARDS = NX * NZ
KEEP = 32
SUB = 24
SEND = SHARDS * SUB
PICK = ROWS + 2 * TOK
PAY = 8 + KEEP
SLAB = NZ * TOK
FACTOR = math.log2(math.e) / math.sqrt(HD)
LOW = -1e30
NT = (((1,), (1,)), ((), ()))
TN = (((0,), (0,)), ((), ()))
VMEM_BYTES = 40 * 1024 * 1024


def smem():
    return pl.BlockSpec(memory_space=pltpu.SMEM)


def vmem():
    return pl.BlockSpec(memory_space=pltpu.VMEM)


def params():
    return pltpu.CompilerParams(vmem_limit_bytes=VMEM_BYTES)


def wide(column):
    return jnp.broadcast_to(column, (column.shape[0], 128))


def tiled(array, count):
    return jnp.concatenate([array] * count, axis=1)


def keys_of(ref):
    return ref[:, 0].reshape(-1, HD)


def values_of(ref):
    value = ref[:, 1].reshape(-1, HD)
    return jnp.concatenate([value, jnp.ones_like(value)], axis=1)


def flash(query, key, value, old, weights_ref, rows, allowed=None):
    count = key.shape[0] // TOK
    scores = lax.dot_general(query, key, NT, preferred_element_type=jnp.float32)
    if allowed is not None:
        scores = jnp.where(allowed, scores, LOW)
    best = scores[:, 0:TOK]
    for i in range(1, count):
        best = jnp.maximum(best, scores[:, i * TOK : (i + 1) * TOK])
    top = wide(jnp.max(best, axis=1, keepdims=True))
    if old is not None:
        top = jnp.maximum(old[0], top)
    weights = jnp.exp2((scores - tiled(top, count)) * FACTOR).astype(jnp.bfloat16)
    weights_ref[rows] = weights
    both = jnp.dot(weights, value, preferred_element_type=jnp.float32)
    mixed, total = both[:, :HD], both[:, HD:]
    if old is not None:
        shrink = jnp.exp2((old[0] - top) * FACTOR)
        total = total + old[1] * shrink
        mixed = mixed + old[2] * shrink
    return top, total, mixed


def flash_heads(q_ref, key, value, state, weights_ref, fresh=False, allowed=None):
    for h in range(GROUP):
        rows = slice(h * TOK, (h + 1) * TOK)
        query = q_ref[:, h * HD : (h + 1) * HD]
        old = None if fresh else tuple(ref[rows] for ref in state)
        for ref, part in zip(state, flash(query, key, value, old, weights_ref, rows, allowed)):
            ref[rows] = part


def own_kernel(place_ref, q_ref, slab_ref, top_ref, total_ref, mixed_ref, weights_ref):
    token = lax.broadcasted_iota(jnp.int32, (TOK, SLAB), 0)
    key = lax.broadcasted_iota(jnp.int32, (TOK, SLAB), 1)
    flash_heads(
        q_ref,
        keys_of(slab_ref),
        values_of(slab_ref),
        (top_ref, total_ref, mixed_ref),
        weights_ref,
        fresh=True,
        allowed=key - token <= place_ref[1] * TOK,
    )


def pick_kernel(slot_row_ref, pick_ref):
    slot_row = slot_row_ref[...]
    target_row = jnp.where(slot_row >= 0, slot_row >> 5, -1)
    target_col = jnp.transpose(jnp.broadcast_to(target_row, (TOK, TOK)))
    first = lax.broadcasted_iota(jnp.int32, (TOK, TOK), 0)
    second = lax.broadcasted_iota(jnp.int32, (TOK, TOK), 1)
    earlier = jnp.where((target_col == target_row) & (first < second), 1, 0)
    rank = jnp.sum(earlier, axis=0, keepdims=True)
    placed = jnp.where(target_row >= 0, target_row * 2 + rank, -1)[None]
    shape = (SHARDS, SUB, TOK)
    to = lax.broadcasted_iota(jnp.int32, shape, 0)
    sub = lax.broadcasted_iota(jnp.int32, shape, 1)
    lane = lax.broadcasted_iota(jnp.int32, shape, 2)
    head = jnp.where(sub < 16, sub & 7, -1)
    same = placed == to * 2 + (sub >> 3)

    def put(at, hit):
        picked = jnp.where(hit, 1.0, 0.0).reshape(SEND, TOK)
        pick_ref[:, at : at + TOK] = picked.astype(jnp.bfloat16)

    for h in range(GROUP):
        put(h * TOK, same & (head == h))
    put(ROWS, (placed == to * 2 + (sub - 18)) & ((sub == 18) | (sub == 19)))
    put(ROWS + TOK, lane == jnp.where(sub == 16, to, jnp.where(sub == 17, to + SHARDS, -1)))


def next_kernel(
    place_ref,
    q_ref,
    left_ref,
    right_ref,
    top_in,
    total_in,
    mixed_in,
    top_ref,
    total_ref,
    mixed_ref,
    top_left_ref,
    weights_left_ref,
    weights_right_ref,
):
    x = place_ref[0]
    state = (top_ref, total_ref, mixed_ref)
    for ref, old in zip(state, (top_in, total_in, mixed_in)):
        ref[...] = old[...]

    @pl.when(x > 0)
    def _():
        flash_heads(q_ref, keys_of(left_ref), values_of(left_ref), state, weights_left_ref)

    top_left_ref[...] = top_ref[...]

    @pl.when(x == NX - 1)
    def _():
        flash_heads(q_ref, keys_of(right_ref), values_of(right_ref), state, weights_right_ref)


def last_kernel(
    place_ref,
    q_ref,
    far_left_ref,
    far_right_ref,
    text_ref,
    slots_ref,
    pick_ref,
    top_in,
    total_in,
    mixed_in,
    top_own_ref,
    top_left_ref,
    weights_own_ref,
    weights_left_ref,
    weights_right_ref,
    context_ref,
    send_ref,
    top_ref,
    total_ref,
    mixed_ref,
    weights_far_ref,
    mass_ref,
):
    x = place_ref[0]
    state = (top_ref, total_ref, mixed_ref)
    for ref, old in zip(state, (top_in, total_in, mixed_in)):
        ref[...] = old[...]
    mass_ref[...] = jnp.zeros_like(mass_ref)

    @pl.when(x >= 2)
    def _():
        key = jnp.concatenate([keys_of(far_left_ref), keys_of(far_right_ref)], axis=0)
        value = jnp.concatenate([values_of(far_left_ref), values_of(far_right_ref)], axis=0)
        flash_heads(q_ref, key, value, state, weights_far_ref)

    context = (mixed_ref[...] / total_ref[...]).astype(jnp.bfloat16)
    for h in range(GROUP):
        context_ref[:, h * HD : (h + 1) * HD] = context[h * TOK : (h + 1) * TOK]

    text = text_ref[...].astype(jnp.float32)

    @pl.when(place_ref[2] > 0)
    def _():
        eye = lax.broadcasted_iota(jnp.int32, (TOK, TOK), 0) == lax.broadcasted_iota(
            jnp.int32, (TOK, TOK), 1
        )

        def mass_of(top_then_ref, weights_ref, at):
            shares = []
            for h in range(GROUP):
                rows = slice(h * TOK, (h + 1) * TOK)
                share = jnp.exp2((top_then_ref[rows] - top_ref[rows]) * FACTOR) / total_ref[rows]
                share = jnp.sum(jnp.where(eye, share, 0.0), axis=0, keepdims=True)
                shares.append(share * text)
            share = jnp.concatenate(shares, axis=1)
            high = share.astype(jnp.bfloat16).astype(jnp.float32)
            low = share - high
            both = jnp.concatenate(
                [jnp.broadcast_to(high, (8, ROWS)), jnp.broadcast_to(low, (8, ROWS))], axis=0
            ).astype(jnp.bfloat16)
            added = jnp.dot(both, weights_ref[...], preferred_element_type=jnp.float32)
            added = added[0:1] + added[8:9]
            shift = lax.rem(at, NX) * NZ
            for i in range(NZ):
                mass_ref[pl.ds(shift + i, 1), :] = added[:, i * TOK : (i + 1) * TOK]

        mass_of(top_own_ref, weights_own_ref, x)

        @pl.when(x > 0)
        def _():
            mass_of(top_left_ref, weights_left_ref, x + NX - 1)

        @pl.when(x == NX - 1)
        def _():
            mass_of(top_in, weights_right_ref, x + 1)

        @pl.when(x >= 2)
        def _():
            mass_of(top_ref, weights_far_ref, x + 2)

    mass = mass_ref[...]
    high = mass.astype(jnp.bfloat16).astype(jnp.float32)
    low = mass - high
    both = jnp.concatenate([high, low, jnp.zeros((TOK - 2 * SHARDS, HD), jnp.float32)], axis=0)
    slots = slots_ref[...]
    slots = jnp.where(slots >= 0, (slots & (KEEP - 1)) + 1, 0).astype(jnp.float32)
    source = jnp.concatenate(
        [context, slots.astype(jnp.bfloat16), both.astype(jnp.bfloat16)], axis=0
    )
    send_ref[...] = jnp.dot(pick_ref[...], source, preferred_element_type=jnp.float32).astype(
        jnp.bfloat16
    )


def place_kernel(got_ref, rows_ref, pay_ref):
    got = got_ref[...].astype(jnp.float32).reshape(SHARDS, SUB, HD)
    mass = jnp.sum(got[:, 16:17, :] + got[:, 17:18, :], axis=0)
    slots = jnp.concatenate(
        [
            jnp.broadcast_to(got[:, 18:19, :], (SHARDS, 8, HD)),
            jnp.broadcast_to(got[:, 19:20, :], (SHARDS, 8, HD)),
            jnp.zeros((SHARDS, 8, HD), jnp.float32),
        ],
        axis=1,
    ).astype(jnp.int32)
    shape = (SHARDS, SUB, HD)
    head = lax.broadcasted_iota(jnp.int32, shape, 1) & 7
    lane = lax.broadcasted_iota(jnp.int32, shape, 2)
    parts = []
    for half in range(2):
        hit = (slots == (lane & (KEEP - 1)) + 1) & (head == (lane >> 5) + 4 * half)
        parts.append(jnp.where(hit, 1.0, 0.0).reshape(SEND, HD))
    put = jnp.concatenate(parts, axis=1).astype(jnp.bfloat16)
    rows = lax.dot_general(put, got_ref[...], TN, preferred_element_type=jnp.float32)
    rows_ref[...] = rows
    squares = jnp.sum((rows * rows).reshape(GROUP, KEEP, HD), axis=0)
    squares = jnp.sum(squares, axis=1, keepdims=True)
    pay_ref[...] = jnp.concatenate([jnp.broadcast_to(mass, (8, HD)), wide(squares)], axis=0)


def finish_kernel(a_ref, b_ref, c_ref, d_ref, rows_ref, gain_ref, text_ref, mass_ref, kept_ref):
    pay = (a_ref[...] + b_ref[...]) + (c_ref[...] + d_ref[...])
    mass_ref[...] = pay[0:1] * (1.0 - text_ref[...].astype(jnp.float32))
    factor = lax.rsqrt(pay[8:] / D + 1e-06)
    for h in range(GROUP):
        columns = slice(h * HD, (h + 1) * HD)
        kept_ref[:, columns] = (
            rows_ref[h * KEEP : (h + 1) * KEEP] * factor * gain_ref[:, columns]
        ).astype(jnp.bfloat16)


def shape_of(shape, dtype):
    return jax.ShapeDtypeStruct(shape, dtype)


def shifted(value, axis, step, count):
    return lax.ppermute(value, axis, [(i, (i + step) % count) for i in range(count)])


def cost(flops):
    return pl.CostEstimate(flops=flops, bytes_accessed=2**10, transcendentals=0)


def on_device(queries, key_rows, value_rows, text_mask, kept_slot, norm_gain):
    f32, bf16 = jnp.float32, jnp.bfloat16
    x = lax.axis_index("x")
    z = lax.axis_index("z")
    place = jnp.stack([x, z, jnp.max(text_mask)]).astype(jnp.int32)
    slot_columns = jnp.broadcast_to(kept_slot[:, None], (TOK, HD))

    both = jnp.stack([key_rows, value_rows])
    own = lax.all_to_all(
        jnp.broadcast_to(both[None], (NZ, 2, TOK, HD)), "z", split_axis=0, concat_axis=0, tiled=True
    )
    left = shifted(own, "x", 1, NX)
    right = shifted(own, "x", -1, NX)
    state = [shape_of((ROWS, HD), f32)] * 3
    kept_weights = shape_of((ROWS, SLAB), bf16)
    pick = pl.pallas_call(
        pick_kernel,
        in_specs=[vmem()],
        out_specs=vmem(),
        out_shape=shape_of((SEND, PICK), bf16),
        compiler_params=params(),
        cost_estimate=cost(5 * 10**8),
        name="pick",
    )(kept_slot[None])
    top_own, total, mixed, weights_own = pl.pallas_call(
        own_kernel,
        in_specs=[smem(), vmem(), vmem()],
        out_specs=[vmem()] * 4,
        out_shape=state + [kept_weights],
        compiler_params=params(),
        cost_estimate=cost(2 * 10**9),
        name="own_slab",
    )(place, queries, own)
    left, right, top_own, pick = lax.optimization_barrier((left, right, top_own, pick))
    half = NZ // 2
    far_left = shifted(left[:half], "x", 1, NX)
    far_right = shifted(right[half:], "x", -1, NX)
    top, total, mixed, top_left, weights_left, weights_right = pl.pallas_call(
        next_kernel,
        in_specs=[smem()] + [vmem()] * 6,
        out_specs=[vmem()] * 6,
        out_shape=state + [state[0]] + [kept_weights] * 2,
        compiler_params=params(),
        cost_estimate=cost(4 * 10**9),
        name="next_slabs",
    )(place, queries, left, right, top_own, total, mixed)
    context, send = pl.pallas_call(
        last_kernel,
        in_specs=[smem()] + [vmem()] * 14,
        out_specs=[vmem()] * 2,
        out_shape=[shape_of((TOK, GROUP * HD), bf16), shape_of((SEND, HD), bf16)],
        scratch_shapes=[pltpu.VMEM((ROWS, HD), f32)] * 3
        + [pltpu.VMEM((ROWS, SLAB), bf16), pltpu.VMEM((SHARDS, HD), f32)],
        compiler_params=params(),
        cost_estimate=cost(4 * 10**9),
        name="last_slab",
    )(
        place, queries, far_left, far_right, text_mask[None], slot_columns, pick,
        top, total, mixed, top_own, top_left, weights_own, weights_left, weights_right,
    )
    got = lax.all_to_all(
        send.reshape(SHARDS, SUB, HD), ("x", "z"), split_axis=0, concat_axis=0, tiled=True
    ).reshape(SEND, HD)
    rows, pay = pl.pallas_call(
        place_kernel,
        in_specs=[vmem()],
        out_specs=[vmem()] * 2,
        out_shape=[shape_of((GROUP * KEEP, HD), f32), shape_of((PAY, HD), f32)],
        compiler_params=params(),
        name="place_rows",
    )(got)
    pay = pay + shifted(pay, "core", 1, 2)
    pays = [pay] + [shifted(pay, "y", step, 4) for step in (1, 2, 3)]
    mass, kept = pl.pallas_call(
        finish_kernel,
        in_specs=[vmem()] * 7,
        out_specs=[vmem()] * 2,
        out_shape=[shape_of((1, TOK), f32), shape_of((KEEP, GROUP * HD), bf16)],
        compiler_params=params(),
        name="finish",
    )(*pays, rows, norm_gain[None], text_mask[None])
    return context, mass[0], kept


def solution(mesh):
    cut = Mesh(mesh.devices.reshape(NX, NZ, 4, 2), ("x", "z", "y", "core"))
    seq, tp = ("x", "z"), ("y", "core")
    placed = (P(seq, tp), P(seq, tp), P(seq, tp), P(seq), P(seq), P(tp))
    return jax.shard_map(
        on_device,
        mesh=cut,
        in_specs=placed,
        out_specs=(P(seq, tp), P(seq), P(seq, tp)),
        check_vma=False,
    )
```

```python
import math

import jax
import jax.numpy as jnp
from jax import lax
from jax.experimental import pallas as pl
from jax.experimental.pallas import tpu as pltpu
from jax.sharding import Mesh, PartitionSpec as P

HD = 128
D = 8192
TOK = 128
GROUP = 8
ROWS = GROUP * TOK
NX = 4
NZ = 8
SHARDS = NX * NZ
KEEP = 32
SUB = 24
SEND = SHARDS * SUB
EIGHT = SHARDS * 8
TP = 8
SLAB = NZ * TOK
FACTOR = math.log2(math.e) / math.sqrt(HD)
LOW = -1e30
NT = (((1,), (1,)), ((), ()))
TN = (((0,), (0,)), ((), ()))
VMEM_BYTES = 40 * 1024 * 1024


def smem():
    return pl.BlockSpec(memory_space=pltpu.SMEM)


def vmem():
    return pl.BlockSpec(memory_space=pltpu.VMEM)


def params():
    return pltpu.CompilerParams(vmem_limit_bytes=VMEM_BYTES)


def wide(column):
    return jnp.broadcast_to(column, (column.shape[0], 128))


def tiled(array, count):
    return jnp.concatenate([array] * count, axis=1)


def diagonal(rows=TOK):
    return lax.broadcasted_iota(jnp.int32, (rows, TOK), 0) == lax.broadcasted_iota(
        jnp.int32, (rows, TOK), 1
    )


def row_of(column, eye):
    return jnp.sum(jnp.where(eye, column, 0.0), axis=0, keepdims=True)


def rows_of(ref, eye):
    return jnp.concatenate(
        [row_of(ref[h * TOK : (h + 1) * TOK], eye) for h in range(GROUP)], axis=0
    )


def keys_of(same_ref, other_ref):
    return jnp.concatenate([ref[:, 0].reshape(-1, HD) for ref in (same_ref, other_ref)], axis=0)


def values_of(same_ref, other_ref):
    value = jnp.concatenate(
        [ref[:, 1].reshape(-1, HD) for ref in (same_ref, other_ref)], axis=0
    )
    return jnp.concatenate([value, jnp.ones_like(value)], axis=1)


def shard_of(chunk, z):
    parity = z & 1
    return 2 * (chunk & 3) + jnp.where(chunk < 4, parity, 1 - parity)


def flash(query, key, value, old, weights_ref, rows, allowed=None):
    count = key.shape[0] // TOK
    scores = lax.dot_general(query, key, NT, preferred_element_type=jnp.float32)
    if allowed is not None:
        scores = jnp.where(allowed, scores, LOW)
    best = scores[:, 0:TOK]
    for i in range(1, count):
        best = jnp.maximum(best, scores[:, i * TOK : (i + 1) * TOK])
    top = wide(jnp.max(best, axis=1, keepdims=True))
    if old is not None:
        top = jnp.maximum(old[0], top)
    weights = jnp.exp2((scores - tiled(top, count)) * FACTOR).astype(jnp.bfloat16)
    weights_ref[rows] = weights
    both = jnp.dot(weights, value, preferred_element_type=jnp.float32)
    mixed, total = both[:, :HD], both[:, HD:]
    if old is not None:
        shrink = jnp.exp2((old[0] - top) * FACTOR)
        total = total + old[1] * shrink
        mixed = mixed + old[2] * shrink
    return top, total, mixed


def flash_heads(q_ref, key, value, state, weights_ref, fresh=False, allowed=None):
    for h in range(GROUP):
        rows = slice(h * TOK, (h + 1) * TOK)
        query = q_ref[:, h * HD : (h + 1) * HD]
        old = None if fresh else tuple(ref[rows] for ref in state)
        for ref, part in zip(state, flash(query, key, value, old, weights_ref, rows, allowed)):
            ref[rows] = part


def own_kernel(
    place_ref,
    q_ref,
    same_ref,
    other_ref,
    top_ref,
    total_ref,
    mixed_ref,
    level_ref,
    weights_ref,
):
    z = place_ref[1]
    token = lax.broadcasted_iota(jnp.int32, (TOK, SLAB), 0)
    lane = lax.broadcasted_iota(jnp.int32, (TOK, SLAB), 1)
    key = shard_of(lane >> 7, z) * TOK + (lane & (TOK - 1))
    flash_heads(
        q_ref,
        keys_of(same_ref, other_ref),
        values_of(same_ref, other_ref),
        (top_ref, total_ref, mixed_ref),
        weights_ref,
        fresh=True,
        allowed=key - token <= z * TOK,
    )
    level_ref[...] = rows_of(top_ref, diagonal())


def pick_kernel(slot_row_ref, rows_ref, rest_ref):
    slot_row = slot_row_ref[...]
    target_row = jnp.where(slot_row >= 0, slot_row >> 5, -1)
    target_col = jnp.transpose(jnp.broadcast_to(target_row, (TOK, TOK)))
    first = lax.broadcasted_iota(jnp.int32, (TOK, TOK), 0)
    second = lax.broadcasted_iota(jnp.int32, (TOK, TOK), 1)
    earlier = jnp.where((target_col == target_row) & (first < second), 1, 0)
    rank = jnp.sum(earlier, axis=0, keepdims=True)
    placed = jnp.where(target_row >= 0, target_row * 2 + rank, -1)[None]
    shape = (SHARDS, 8, TOK)
    to = lax.broadcasted_iota(jnp.int32, shape, 0)
    sub = lax.broadcasted_iota(jnp.int32, shape, 1)
    lane = lax.broadcasted_iota(jnp.int32, shape, 2)

    def one_hot(hit):
        return jnp.where(hit, 1.0, 0.0).reshape(EIGHT, TOK).astype(jnp.bfloat16)

    same = placed == to * 2 + (sub >> 2)
    for h in range(4):
        rows_ref[:, h * TOK : (h + 1) * TOK] = one_hot(same & ((sub & 3) == h))
    rest_ref[:, :TOK] = one_hot((placed == to * 2 + (sub - 2)) & ((sub == 2) | (sub == 3)))
    rest_ref[:, TOK:] = one_hot(lane == jnp.where(sub == 0, to, jnp.where(sub == 1, to + SHARDS, -1)))


def next_kernel(
    place_ref,
    q_ref,
    left_same_ref,
    left_other_ref,
    right_same_ref,
    right_other_ref,
    top_in,
    total_in,
    mixed_in,
    top_ref,
    total_ref,
    mixed_ref,
    level_left_ref,
    level_right_ref,
    weights_left_ref,
    weights_right_ref,
):
    x = place_ref[0]
    eye = diagonal()
    state = (top_ref, total_ref, mixed_ref)
    for ref, old in zip(state, (top_in, total_in, mixed_in)):
        ref[...] = old[...]

    @pl.when(x > 0)
    def _():
        pair = (left_same_ref, left_other_ref)
        flash_heads(q_ref, keys_of(*pair), values_of(*pair), state, weights_left_ref)

    level_left_ref[...] = rows_of(top_ref, eye)

    @pl.when(x == NX - 1)
    def _():
        pair = (right_same_ref, right_other_ref)
        flash_heads(q_ref, keys_of(*pair), values_of(*pair), state, weights_right_ref)

    level_right_ref[...] = rows_of(top_ref, eye)


def last_kernel(
    place_ref,
    q_ref,
    far_same_ref,
    far_other_ref,
    text_ref,
    slots_ref,
    pick_rows_ref,
    pick_rest_ref,
    top_in,
    total_in,
    mixed_in,
    level_own_ref,
    level_left_ref,
    level_right_ref,
    weights_own_ref,
    weights_left_ref,
    weights_right_ref,
    context_ref,
    send_ref,
    top_ref,
    total_ref,
    mixed_ref,
    weights_far_ref,
    mass_ref,
):
    x = place_ref[0]
    state = (top_ref, total_ref, mixed_ref)
    for ref, old in zip(state, (top_in, total_in, mixed_in)):
        ref[...] = old[...]
    mass_ref[...] = jnp.zeros_like(mass_ref)

    @pl.when(x >= 2)
    def _():
        pair = (far_same_ref, far_other_ref)
        flash_heads(q_ref, keys_of(*pair), values_of(*pair), state, weights_far_ref)

    context = (mixed_ref[...] / total_ref[...]).astype(jnp.bfloat16)
    for h in range(GROUP):
        context_ref[:, h * HD : (h + 1) * HD] = context[h * TOK : (h + 1) * TOK]

    @pl.when(place_ref[2] > 0)
    def _():
        eye = diagonal()
        level = rows_of(top_ref, eye)
        part = text_ref[...].astype(jnp.float32) / rows_of(total_ref, eye)

        def mass_of(level_then, weights_ref, at):
            share = jnp.exp2((level_then - level) * FACTOR) * part
            share = jnp.concatenate([share[h : h + 1] for h in range(GROUP)], axis=1)
            high = share.astype(jnp.bfloat16).astype(jnp.float32)
            low = share - high
            both = jnp.concatenate(
                [jnp.broadcast_to(high, (8, ROWS)), jnp.broadcast_to(low, (8, ROWS))], axis=0
            ).astype(jnp.bfloat16)
            added = jnp.dot(both, weights_ref[...], preferred_element_type=jnp.float32)
            added = added[0:1] + added[8:9]
            shift = lax.rem(at, NX) * NZ
            for i in range(NZ):
                to = shift + shard_of(i, place_ref[1])
                mass_ref[pl.ds(to, 1), :] = added[:, i * TOK : (i + 1) * TOK]

        mass_of(level_own_ref[...], weights_own_ref, x)

        @pl.when(x > 0)
        def _():
            mass_of(level_left_ref[...], weights_left_ref, x + NX - 1)

        @pl.when(x == NX - 1)
        def _():
            mass_of(level_right_ref[...], weights_right_ref, x + 1)

        @pl.when(x >= 2)
        def _():
            mass_of(level, weights_far_ref, x + 2)

    half = ROWS // 2
    sides = jnp.concatenate([context[:half], context[half:]], axis=1)
    sides = jnp.dot(pick_rows_ref[...], sides, preferred_element_type=jnp.float32)
    mass = mass_ref[...]
    high = mass.astype(jnp.bfloat16).astype(jnp.float32)
    low = mass - high
    slots = slots_ref[...]
    slots = jnp.where(slots >= 0, (slots & (KEEP - 1)) + 1, 0).astype(jnp.float32)
    rest = jnp.concatenate(
        [slots, high, low, jnp.zeros((TOK - 2 * SHARDS, HD), jnp.float32)], axis=0
    )
    rest = jnp.dot(
        pick_rest_ref[...], rest.astype(jnp.bfloat16), preferred_element_type=jnp.float32
    )
    parts = [part.reshape(SHARDS, 8, HD) for part in (sides[:, :HD], sides[:, HD:], rest)]
    send = jnp.concatenate(parts, axis=1).reshape(SEND, HD)
    send_ref[...] = send.astype(jnp.bfloat16)


def place_kernel(got_ref, rows_ref, pay_ref):
    got = got_ref[...].astype(jnp.float32).reshape(SHARDS, SUB, HD)
    mass = jnp.sum(got[:, 16:17, :] + got[:, 17:18, :], axis=0)
    slots = jnp.concatenate(
        [
            jnp.broadcast_to(got[:, 18:19, :], (SHARDS, 4, HD)),
            jnp.broadcast_to(got[:, 19:20, :], (SHARDS, 4, HD)),
        ],
        axis=1,
    ).astype(jnp.int32)
    shape = (SHARDS, 8, HD)
    head = lax.broadcasted_iota(jnp.int32, shape, 1) & 3
    lane = lax.broadcasted_iota(jnp.int32, shape, 2)
    hit = (slots == (lane & (KEEP - 1)) + 1) & (head == lane >> 5)
    put = jnp.where(hit, 1.0, 0.0).reshape(EIGHT, HD).astype(jnp.bfloat16)
    sides = jnp.concatenate(
        [got[:, 0:8].reshape(EIGHT, HD), got[:, 8:16].reshape(EIGHT, HD)], axis=1
    ).astype(jnp.bfloat16)
    rows = lax.dot_general(put, sides, TN, preferred_element_type=jnp.float32)
    rows_ref[...] = rows
    squares = jnp.sum((rows * rows).reshape(4, KEEP, 2 * HD), axis=0)
    squares = jnp.sum(squares, axis=1, keepdims=True)
    squares = row_of(wide(squares), diagonal(KEEP))
    pay = jnp.concatenate([mass, squares, jnp.zeros((6, HD), jnp.float32)], axis=0)
    pay_ref[...] = jnp.broadcast_to(pay[None], (TP, 8, HD))


def finish_kernel(pay_ref, rows_ref, gain_ref, text_ref, mass_ref, kept_ref):
    pay = jnp.sum(pay_ref[...], axis=0)
    mass_ref[...] = pay[0:1] * (1.0 - text_ref[...].astype(jnp.float32))
    squares = jnp.where(diagonal(KEEP), jnp.broadcast_to(pay[1:2], (KEEP, HD)), 0.0)
    factor = lax.rsqrt(wide(jnp.sum(squares, axis=1, keepdims=True)) / D + 1e-06)
    for h in range(GROUP):
        columns = slice(h * HD, (h + 1) * HD)
        rows = slice((h & 3) * KEEP, ((h & 3) + 1) * KEEP)
        side = slice((h >> 2) * HD, ((h >> 2) + 1) * HD)
        kept_ref[:, columns] = (rows_ref[rows, side] * factor * gain_ref[:, columns]).astype(
            jnp.bfloat16
        )


def shape_of(shape, dtype):
    return jax.ShapeDtypeStruct(shape, dtype)


def shifted(value, axis, step, count):
    return lax.ppermute(value, axis, [(i, (i + step) % count) for i in range(count)])


def cost(flops):
    return pl.CostEstimate(flops=flops, bytes_accessed=2**10, transcendentals=0)


def on_device(queries, key_rows, value_rows, text_mask, kept_slot, norm_gain):
    f32, bf16 = jnp.float32, jnp.bfloat16
    x = lax.axis_index("x")
    z = lax.axis_index(("zh", "zl"))
    place = jnp.stack([x, z, jnp.max(text_mask)]).astype(jnp.int32)
    slot_columns = jnp.broadcast_to(kept_slot[:, None], (TOK, HD))

    both = jnp.stack([key_rows, value_rows])
    same = lax.all_to_all(
        jnp.broadcast_to(both[None], (NZ // 2, 2, TOK, HD)),
        "zh",
        split_axis=0,
        concat_axis=0,
        tiled=True,
    )
    other = shifted(same, "zl", 1, 2)
    left = [shifted(part, "x", 1, NX) for part in (same, other)]
    right = [shifted(part, "x", -1, NX) for part in (same, other)]
    far = [shifted(left[0], "x", 1, NX), shifted(right[1], "x", -1, NX)]
    state = [shape_of((ROWS, HD), f32)] * 3
    kept_weights = shape_of((ROWS, SLAB), bf16)
    level = shape_of((GROUP, TOK), f32)
    pick = pl.pallas_call(
        pick_kernel,
        in_specs=[vmem()],
        out_specs=[vmem()] * 2,
        out_shape=[shape_of((EIGHT, 4 * TOK), bf16), shape_of((EIGHT, 2 * TOK), bf16)],
        compiler_params=params(),
        cost_estimate=cost(5 * 10**8),
        name="pick",
    )(kept_slot[None])
    top, total, mixed, level_own, weights_own = pl.pallas_call(
        own_kernel,
        in_specs=[smem()] + [vmem()] * 3,
        out_specs=[vmem()] * 5,
        out_shape=state + [level, kept_weights],
        compiler_params=params(),
        cost_estimate=cost(2 * 10**9),
        name="own_slab",
    )(place, queries, same, other)
    top, total, mixed, level_left, level_right, weights_left, weights_right = pl.pallas_call(
        next_kernel,
        in_specs=[smem()] + [vmem()] * 8,
        out_specs=[vmem()] * 7,
        out_shape=state + [level] * 2 + [kept_weights] * 2,
        compiler_params=params(),
        cost_estimate=cost(4 * 10**9),
        name="next_slabs",
    )(place, queries, *left, *right, top, total, mixed)
    context, send = pl.pallas_call(
        last_kernel,
        in_specs=[smem()] + [vmem()] * 16,
        out_specs=[vmem()] * 2,
        out_shape=[shape_of((TOK, GROUP * HD), bf16), shape_of((SEND, HD), bf16)],
        scratch_shapes=[pltpu.VMEM((ROWS, HD), f32)] * 3
        + [pltpu.VMEM((ROWS, SLAB), bf16), pltpu.VMEM((SHARDS, HD), f32)],
        compiler_params=params(),
        cost_estimate=cost(4 * 10**9),
        name="last_slab",
    )(
        place, queries, *far, text_mask[None], slot_columns, *pick,
        top, total, mixed, level_own, level_left, level_right,
        weights_own, weights_left, weights_right,
    )
    got = lax.all_to_all(
        send.reshape(SHARDS, SUB, HD), ("x", "zh", "zl"), split_axis=0, concat_axis=0, tiled=True
    ).reshape(SEND, HD)
    rows, pay = pl.pallas_call(
        place_kernel,
        in_specs=[vmem()],
        out_specs=[vmem()] * 2,
        out_shape=[shape_of((4 * KEEP, 2 * HD), f32), shape_of((TP, 8, HD), f32)],
        compiler_params=params(),
        name="place_rows",
    )(got)
    pay = lax.all_to_all(pay, ("y", "core"), split_axis=0, concat_axis=0, tiled=True)
    mass, kept = pl.pallas_call(
        finish_kernel,
        in_specs=[vmem()] * 4,
        out_specs=[vmem()] * 2,
        out_shape=[shape_of((1, TOK), f32), shape_of((KEEP, GROUP * HD), bf16)],
        compiler_params=params(),
        name="finish",
    )(pay, rows, norm_gain[None], text_mask[None])
    return context, mass[0], kept


def solution(mesh):
    cut = Mesh(mesh.devices.reshape(NX, NZ // 2, 2, 4, 2), ("x", "zh", "zl", "y", "core"))
    seq, tp = ("x", "zh", "zl"), ("y", "core")
    placed = (P(seq, tp), P(seq, tp), P(seq, tp), P(seq), P(seq), P(tp))
    return jax.shard_map(
        on_device,
        mesh=cut,
        in_specs=placed,
        out_specs=(P(seq, tp), P(seq), P(seq, tp)),
        check_vma=False,
    )
```

```python
import math

import jax
import jax.numpy as jnp
from jax import lax
from jax.experimental import pallas as pl
from jax.experimental.pallas import tpu as pltpu
from jax.sharding import Mesh, PartitionSpec as P

HD = 128
D = 8192
TOK = 128
GROUP = 8
ROWS = GROUP * TOK
NX = 4
NZ = 8
SHARDS = NX * NZ
KEEP = 32
SUB = 24
SEND = SHARDS * SUB
EIGHT = SHARDS * 8
TP = 8
PART = NZ * TOK // 2
FACTOR = math.log2(math.e) / math.sqrt(HD)
LOW = -1e30
NT = (((1,), (1,)), ((), ()))
TN = (((0,), (0,)), ((), ()))
VMEM_BYTES = 40 * 1024 * 1024


def vmem():
    return pl.BlockSpec(memory_space=pltpu.VMEM)


def params():
    return pltpu.CompilerParams(vmem_limit_bytes=VMEM_BYTES)


def wide(column):
    return jnp.broadcast_to(column, (column.shape[0], 128))


def tiled(array, count):
    return jnp.concatenate([array] * count, axis=1)


def position():
    return lax.axis_index("x"), lax.axis_index("zh") * 2 + lax.axis_index("zl")


def diagonal(rows=TOK):
    return lax.broadcasted_iota(jnp.int32, (rows, TOK), 0) == lax.broadcasted_iota(
        jnp.int32, (rows, TOK), 1
    )


def row_of(column, eye):
    return jnp.sum(jnp.where(eye, column, 0.0), axis=0, keepdims=True)


def rows_of(ref, eye):
    return jnp.concatenate(
        [row_of(ref[h * TOK : (h + 1) * TOK], eye) for h in range(GROUP)], axis=0
    )


def keys_of(*refs):
    return jnp.concatenate([ref[:, 0].reshape(-1, HD) for ref in refs], axis=0)


def values_of(*refs):
    value = jnp.concatenate([ref[:, 1].reshape(-1, HD) for ref in refs], axis=0)
    return jnp.concatenate([value, jnp.ones_like(value)], axis=1)


def shard_of(chunk, z):
    parity = z & 1
    return 2 * (chunk & 3) + jnp.where(chunk < 4, parity, 1 - parity)


def flash(query, key, value, old, weights_ref, rows, allowed=None):
    count = key.shape[0] // TOK
    scores = lax.dot_general(query, key, NT, preferred_element_type=jnp.float32)
    if allowed is not None:
        scores = jnp.where(allowed, scores, LOW)
    best = scores[:, 0:TOK]
    for i in range(1, count):
        best = jnp.maximum(best, scores[:, i * TOK : (i + 1) * TOK])
    top = wide(jnp.max(best, axis=1, keepdims=True))
    if old is not None:
        top = jnp.maximum(old[0], top)
    weights = jnp.exp2((scores - tiled(top, count)) * FACTOR).astype(jnp.bfloat16)
    weights_ref[rows] = weights
    both = jnp.dot(weights, value, preferred_element_type=jnp.float32)
    mixed, total = both[:, :HD], both[:, HD:]
    if old is not None:
        shrink = jnp.exp2((old[0] - top) * FACTOR)
        total = total + old[1] * shrink
        mixed = mixed + old[2] * shrink
    return top, total, mixed


def flash_heads(q_ref, pair, old_state, state, weights_ref, allowed=None):
    key = keys_of(*pair)
    value = values_of(*pair)
    for h in range(GROUP):
        rows = slice(h * TOK, (h + 1) * TOK)
        query = q_ref[:, h * HD : (h + 1) * HD]
        old = None if old_state is None else tuple(ref[rows] for ref in old_state)
        for ref, part in zip(state, flash(query, key, value, old, weights_ref, rows, allowed)):
            ref[rows] = part


def copy_state(old_state, state):
    for ref, old in zip(state, old_state):
        ref[...] = old[...]


def own_part(first, q_ref, keys_ref, old_state, state, level_ref, weights_ref):
    z = position()[1]
    token = lax.broadcasted_iota(jnp.int32, (TOK, PART), 0)
    lane = lax.broadcasted_iota(jnp.int32, (TOK, PART), 1)
    key = shard_of(first + (lane >> 7), z) * TOK + (lane & (TOK - 1))
    flash_heads(q_ref, (keys_ref,), old_state, state, weights_ref, key - token <= z * TOK)
    level_ref[...] = rows_of(state[0], diagonal())


def sides(q_ref, left_ref, right_ref, state, level_refs, weights_refs):
    x = position()[0]
    eye = diagonal()

    @pl.when(x > 0)
    def _():
        flash_heads(q_ref, (left_ref,), state, state, weights_refs[0])

    level_refs[0][...] = rows_of(state[0], eye)

    @pl.when(x == NX - 1)
    def _():
        flash_heads(q_ref, (right_ref,), state, state, weights_refs[1])

    level_refs[1][...] = rows_of(state[0], eye)


def first_kernel(q_ref, keys_ref, slot_row_ref, text_ref, *refs):
    state, (level_ref, weights_ref), picked, text_out_ref = refs[:3], refs[3:5], refs[5:8], refs[8]
    text_out_ref[...] = jnp.broadcast_to(text_ref[...].astype(jnp.float32), (8, TOK))
    own_part(0, q_ref, keys_ref, None, state, level_ref, weights_ref)
    pick(slot_row_ref, *picked)


def second_kernel(q_ref, keys_ref, left_ref, right_ref, *refs):
    old_state, state, levels, weights = refs[:3], refs[3:6], refs[6:9], refs[9:]
    own_part(NZ // 2, q_ref, keys_ref, old_state, state, levels[0], weights[0])
    sides(q_ref, left_ref, right_ref, state, levels[1:], weights[1:])


def third_kernel(q_ref, left_ref, right_ref, far_0_ref, far_1_ref, *refs):
    old_state, state, levels, weights = refs[:3], refs[3:6], refs[6:9], refs[9:]
    copy_state(old_state, state)
    sides(q_ref, left_ref, right_ref, state, levels, weights)

    @pl.when(position()[0] >= 2)
    def _():
        flash_heads(q_ref, (far_0_ref, far_1_ref), state, state, weights[2])

    levels[2][...] = rows_of(state[0], diagonal())


def pick(slot_row_ref, rows_ref, rest_ref, slots_ref):
    slot_row = slot_row_ref[...]
    slot_col = jnp.transpose(jnp.broadcast_to(slot_row, (TOK, TOK)))
    slots = jnp.where(slot_col >= 0, (slot_col & (KEEP - 1)) + 1, 0)
    slots_ref[...] = slots.astype(jnp.float32).astype(jnp.bfloat16)
    target_row = jnp.where(slot_row >= 0, slot_row >> 5, -1)
    target_col = jnp.where(slot_col >= 0, slot_col >> 5, -1)
    first = lax.broadcasted_iota(jnp.int32, (TOK, TOK), 0)
    second = lax.broadcasted_iota(jnp.int32, (TOK, TOK), 1)
    earlier = jnp.where((target_col == target_row) & (first < second), 1, 0)
    rank = jnp.sum(earlier, axis=0, keepdims=True)
    placed = jnp.where(target_row >= 0, target_row * 2 + rank, -1)[None]
    shape = (SHARDS, 8, TOK)
    to = lax.broadcasted_iota(jnp.int32, shape, 0)
    sub = lax.broadcasted_iota(jnp.int32, shape, 1)
    lane = lax.broadcasted_iota(jnp.int32, shape, 2)

    def one_hot(hit):
        return jnp.where(hit, 1.0, 0.0).reshape(EIGHT, TOK).astype(jnp.bfloat16)

    same = placed == to * 2 + (sub >> 2)
    for h in range(4):
        rows_ref[:, h * TOK : (h + 1) * TOK] = one_hot(same & ((sub & 3) == h))
    rest_ref[:, :TOK] = one_hot((placed == to * 2 + (sub - 2)) & ((sub == 2) | (sub == 3)))
    rest_ref[:, TOK:] = one_hot(lane == jnp.where(sub == 0, to, jnp.where(sub == 1, to + SHARDS, -1)))


def last_kernel(
    q_ref,
    far_2_ref,
    far_3_ref,
    text_ref,
    pick_rows_ref,
    pick_rest_ref,
    slots_ref,
    top_in,
    total_in,
    mixed_in,
    *refs,
):
    levels, weights = refs[:7], refs[7:14]
    context_ref, send_ref, top_ref, total_ref, mixed_ref, weights_last_ref, mass_ref = refs[14:]
    x, z = position()
    old_state = (top_in, total_in, mixed_in)
    state = (top_ref, total_ref, mixed_ref)
    mass_ref[...] = jnp.zeros_like(mass_ref)

    @pl.when(x >= 2)
    def _():
        flash_heads(q_ref, (far_2_ref, far_3_ref), old_state, state, weights_last_ref)

    @pl.when(x < 2)
    def _():
        copy_state(old_state, state)

    context = (mixed_ref[...] / total_ref[...]).astype(jnp.bfloat16)
    for h in range(GROUP):
        context_ref[:, h * HD : (h + 1) * HD] = context[h * TOK : (h + 1) * TOK]

    text = text_ref[...]

    @pl.when(jnp.max(text) > 0.0)
    def _():
        eye = diagonal()
        level = rows_of(top_ref, eye)
        part = text / rows_of(total_ref, eye)

        def mass_of(level_then, weights_ref, at, first=0):
            share = jnp.exp2((level_then - level) * FACTOR) * part
            share = jnp.concatenate([share[h : h + 1] for h in range(GROUP)], axis=1)
            high = share.astype(jnp.bfloat16).astype(jnp.float32)
            low = share - high
            both = jnp.concatenate(
                [jnp.broadcast_to(high, (8, ROWS)), jnp.broadcast_to(low, (8, ROWS))], axis=0
            ).astype(jnp.bfloat16)
            added = jnp.dot(both, weights_ref[...], preferred_element_type=jnp.float32)
            added = added[0:1] + added[8:9]
            shift = lax.rem(at, NX) * NZ
            for i in range(weights_ref.shape[1] // TOK):
                to = shift + shard_of(first + i, z)
                mass_ref[pl.ds(to, 1), :] = added[:, i * TOK : (i + 1) * TOK]

        own, own_other, left, right, left_other, right_other, far = [
            (level_ref[...], weights_ref) for level_ref, weights_ref in zip(levels, weights)
        ]
        mass_of(*own, x)
        mass_of(*own_other, x, NZ // 2)

        @pl.when(x > 0)
        def _():
            mass_of(*left, x + NX - 1)
            mass_of(*left_other, x + NX - 1, NZ // 2)

        @pl.when(x == NX - 1)
        def _():
            mass_of(*right, x + 1)
            mass_of(*right_other, x + 1, NZ // 2)

        @pl.when(x >= 2)
        def _():
            mass_of(*far, x + 2)
            mass_of(level, weights_last_ref, x + 2, NZ // 2)

    half = ROWS // 2
    sides = jnp.concatenate([context[:half], context[half:]], axis=1)
    sides = jnp.dot(pick_rows_ref[...], sides, preferred_element_type=jnp.float32)
    mass = mass_ref[...]
    high = mass.astype(jnp.bfloat16).astype(jnp.float32)
    low = mass - high
    rest = jnp.concatenate([high, low, jnp.zeros((TOK - 2 * SHARDS, HD), jnp.float32)], axis=0)
    rest = jnp.concatenate([slots_ref[...], rest.astype(jnp.bfloat16)], axis=0)
    rest = jnp.dot(pick_rest_ref[...], rest, preferred_element_type=jnp.float32)
    parts = [part.reshape(SHARDS, 8, HD) for part in (sides[:, :HD], sides[:, HD:], rest)]
    send = jnp.concatenate(parts, axis=1).reshape(SEND, HD)
    send_ref[...] = send.astype(jnp.bfloat16)


def place_kernel(got_ref, rows_ref, pay_ref):
    got = got_ref[...].astype(jnp.float32).reshape(SHARDS, SUB, HD)
    mass = jnp.sum(got[:, 16:17, :] + got[:, 17:18, :], axis=0)
    slots = jnp.concatenate(
        [
            jnp.broadcast_to(got[:, 18:19, :], (SHARDS, 4, HD)),
            jnp.broadcast_to(got[:, 19:20, :], (SHARDS, 4, HD)),
        ],
        axis=1,
    ).astype(jnp.int32)
    shape = (SHARDS, 8, HD)
    head = lax.broadcasted_iota(jnp.int32, shape, 1) & 3
    lane = lax.broadcasted_iota(jnp.int32, shape, 2)
    hit = (slots == (lane & (KEEP - 1)) + 1) & (head == lane >> 5)
    put = jnp.where(hit, 1.0, 0.0).reshape(EIGHT, HD).astype(jnp.bfloat16)
    sides = jnp.concatenate(
        [got[:, 0:8].reshape(EIGHT, HD), got[:, 8:16].reshape(EIGHT, HD)], axis=1
    ).astype(jnp.bfloat16)
    rows = lax.dot_general(put, sides, TN, preferred_element_type=jnp.float32)
    rows_ref[...] = rows
    squares = jnp.sum((rows * rows).reshape(4, KEEP, 2 * HD), axis=0)
    squares = jnp.sum(squares, axis=1, keepdims=True)
    squares = row_of(wide(squares), diagonal(KEEP))
    pay = jnp.concatenate([mass, squares, jnp.zeros((6, HD), jnp.float32)], axis=0)
    pay_ref[...] = jnp.broadcast_to(pay[None], (TP, 8, HD))


def finish_kernel(pay_ref, rows_ref, gain_ref, text_ref, mass_ref, kept_ref):
    pay = jnp.sum(pay_ref[...], axis=0)
    mass_ref[...] = pay[0:1] * (1.0 - text_ref[...].astype(jnp.float32))
    squares = jnp.where(diagonal(KEEP), jnp.broadcast_to(pay[1:2], (KEEP, HD)), 0.0)
    factor = lax.rsqrt(wide(jnp.sum(squares, axis=1, keepdims=True)) / D + 1e-06)
    for h in range(GROUP):
        columns = slice(h * HD, (h + 1) * HD)
        rows = slice((h & 3) * KEEP, ((h & 3) + 1) * KEEP)
        side = slice((h >> 2) * HD, ((h >> 2) + 1) * HD)
        kept_ref[:, columns] = (rows_ref[rows, side] * factor * gain_ref[:, columns]).astype(
            jnp.bfloat16
        )


def shape_of(shape, dtype):
    return jax.ShapeDtypeStruct(shape, dtype)


def shifted(value, axis, step, count):
    return lax.ppermute(value, axis, [(i, (i + step) % count) for i in range(count)])


def cost(flops):
    return pl.CostEstimate(flops=flops, bytes_accessed=2**10, transcendentals=0)


def on_device(queries, key_rows, value_rows, text_mask, kept_slot, norm_gain):
    f32, bf16 = jnp.float32, jnp.bfloat16
    both = jnp.stack([key_rows, value_rows])
    same = lax.all_to_all(
        jnp.broadcast_to(both[None], (NZ // 2, 2, TOK, HD)),
        "zh",
        split_axis=0,
        concat_axis=0,
        tiled=True,
    )
    other = shifted(same, "zl", 1, 2)
    state = [shape_of((ROWS, HD), f32)] * 3
    level = shape_of((GROUP, TOK), f32)
    weights = shape_of((ROWS, PART), bf16)

    def kernel(body, name, inputs, out_shape, scratch=()):
        return pl.pallas_call(
            body,
            in_specs=[vmem()] * len(inputs),
            out_specs=[vmem()] * len(out_shape),
            out_shape=out_shape,
            scratch_shapes=list(scratch),
            compiler_params=params(),
            cost_estimate=cost(10**9),
            name=name,
        )(*inputs)

    *now, level_own, weights_own, pick_rows, pick_rest, slots, text = kernel(
        first_kernel,
        "first",
        [queries, same, kept_slot[None], text_mask[None]],
        state
        + [level, weights]
        + [shape_of((EIGHT, 4 * TOK), bf16), shape_of((EIGHT, 2 * TOK), bf16)]
        + [shape_of((TOK, HD), bf16), shape_of((8, TOK), f32)],
    )
    other, now[0] = lax.optimization_barrier((other, now[0]))
    left = [shifted(part, "x", 1, NX) for part in (same, other)]
    right = [shifted(part, "x", -1, NX) for part in (same, other)]
    outs = kernel(
        second_kernel,
        "second",
        [queries, other, left[0], right[0], *now],
        state + [level] * 3 + [weights] * 3,
    )
    now, levels, kept = list(outs[:3]), [level_own, *outs[3:6]], [weights_own, *outs[6:]]
    left[1], right[1], now[0] = lax.optimization_barrier((left[1], right[1], now[0]))
    half = NZ // 4
    far = []
    for i in range(2):
        far.append(shifted(left[i][:half], "x", 1, NX))
        far.append(shifted(right[i][half:], "x", -1, NX))
    outs = kernel(
        third_kernel,
        "third",
        [queries, left[1], right[1], *far[:2], *now],
        state + [level] * 3 + [weights] * 3,
    )
    now, levels, kept = outs[:3], [*levels, *outs[3:6]], [*kept, *outs[6:]]
    context, send = kernel(
        last_kernel,
        "last",
        [queries, *far[2:], text, pick_rows, pick_rest, slots, *now, *levels, *kept],
        [shape_of((TOK, GROUP * HD), bf16), shape_of((SEND, HD), bf16)],
        [pltpu.VMEM((ROWS, HD), f32)] * 3
        + [pltpu.VMEM((ROWS, PART), bf16), pltpu.VMEM((SHARDS, HD), f32)],
    )
    got = lax.all_to_all(
        send.reshape(SHARDS, SUB, HD), ("x", "zh", "zl"), split_axis=0, concat_axis=0, tiled=True
    ).reshape(SEND, HD)
    rows, pay = pl.pallas_call(
        place_kernel,
        in_specs=[vmem()],
        out_specs=[vmem()] * 2,
        out_shape=[shape_of((4 * KEEP, 2 * HD), f32), shape_of((TP, 8, HD), f32)],
        compiler_params=params(),
        name="place_rows",
    )(got)
    pay = lax.all_to_all(pay, ("y", "core"), split_axis=0, concat_axis=0, tiled=True)
    mass, kept = pl.pallas_call(
        finish_kernel,
        in_specs=[vmem()] * 4,
        out_specs=[vmem()] * 2,
        out_shape=[shape_of((1, TOK), f32), shape_of((KEEP, GROUP * HD), bf16)],
        compiler_params=params(),
        name="finish",
    )(pay, rows, norm_gain[None], text_mask[None])
    return context, mass[0], kept


def solution(mesh):
    cut = Mesh(mesh.devices.reshape(NX, NZ // 2, 2, 4, 2), ("x", "zh", "zl", "y", "core"))
    seq, tp = ("x", "zh", "zl"), ("y", "core")
    placed = (P(seq, tp), P(seq, tp), P(seq, tp), P(seq), P(seq), P(tp))
    return jax.shard_map(
        on_device,
        mesh=cut,
        in_specs=placed,
        out_specs=(P(seq, tp), P(seq), P(seq, tp)),
        check_vma=False,
    )
```

```python
import math

import jax
import jax.numpy as jnp
from jax import lax
from jax.experimental import pallas as pl
from jax.experimental.pallas import tpu as pltpu
from jax.sharding import Mesh, PartitionSpec as P

HD = 128
D = 8192
TOK = 128
GROUP = 8
ROWS = GROUP * TOK
NX = 4
NZ = 8
SHARDS = NX * NZ
KEEP = 32
SUB = 24
SEND = SHARDS * SUB
EIGHT = SHARDS * 8
TP = 8
NEAR = (0, -2, 2, 4)
REST = (1, -1, 3, 5)
FACTOR = math.log2(math.e) / math.sqrt(HD)
LOW = -1e30
NT = (((1,), (1,)), ((), ()))
TN = (((0,), (0,)), ((), ()))
VMEM_BYTES = 40 * 1024 * 1024


def vmem():
    return pl.BlockSpec(memory_space=pltpu.VMEM)


def params():
    return pltpu.CompilerParams(vmem_limit_bytes=VMEM_BYTES)


def wide(column):
    return jnp.broadcast_to(column, (column.shape[0], 128))


def tiled(array, count):
    return jnp.concatenate([array] * count, axis=1)


def position():
    return lax.axis_index("x"), lax.axis_index("zh") * 2 + lax.axis_index("zl")


def diagonal(rows=TOK):
    return lax.broadcasted_iota(jnp.int32, (rows, TOK), 0) == lax.broadcasted_iota(
        jnp.int32, (rows, TOK), 1
    )


def row_of(column, eye):
    return jnp.sum(jnp.where(eye, column, 0.0), axis=0, keepdims=True)


def rows_of(ref, eye):
    return jnp.concatenate(
        [row_of(ref[h * TOK : (h + 1) * TOK], eye) for h in range(GROUP)], axis=0
    )


def keys_of(*refs):
    return jnp.concatenate([ref[:, 0].reshape(-1, HD) for ref in refs], axis=0)


def values_of(*refs):
    value = jnp.concatenate([ref[:, 1].reshape(-1, HD) for ref in refs], axis=0)
    return jnp.concatenate([value, jnp.ones_like(value)], axis=1)


def shard_of(z, offset):
    return (z + offset) & (NZ - 1)


def flash(query, key, value, old, weights_ref, rows, allowed=None):
    count = key.shape[0] // TOK
    scores = lax.dot_general(query, key, NT, preferred_element_type=jnp.float32)
    if allowed is not None:
        scores = jnp.where(allowed, scores, LOW)
    best = scores[:, 0:TOK]
    for i in range(1, count):
        best = jnp.maximum(best, scores[:, i * TOK : (i + 1) * TOK])
    top = wide(jnp.max(best, axis=1, keepdims=True))
    if old is not None:
        top = jnp.maximum(old[0], top)
    weights = jnp.exp2((scores - tiled(top, count)) * FACTOR).astype(jnp.bfloat16)
    weights_ref[rows] = weights
    both = jnp.dot(weights, value, preferred_element_type=jnp.float32)
    mixed, total = both[:, :HD], both[:, HD:]
    if old is not None:
        shrink = jnp.exp2((old[0] - top) * FACTOR)
        total = total + old[1] * shrink
        mixed = mixed + old[2] * shrink
    return top, total, mixed


def flash_heads(q_ref, pair, old_state, state, weights_ref, allowed=None):
    key = keys_of(*pair)
    value = values_of(*pair)
    for h in range(GROUP):
        rows = slice(h * TOK, (h + 1) * TOK)
        query = q_ref[:, h * HD : (h + 1) * HD]
        old = None if old_state is None else tuple(ref[rows] for ref in old_state)
        for ref, part in zip(state, flash(query, key, value, old, weights_ref, rows, allowed)):
            ref[rows] = part


def copy_state(old_state, state):
    for ref, old in zip(state, old_state):
        ref[...] = old[...]


def own_part(offsets, q_ref, keys_ref, old_state, state, level_ref, weights_ref):
    z = position()[1]
    token = lax.broadcasted_iota(jnp.int32, (TOK, TOK), 0)
    lane = lax.broadcasted_iota(jnp.int32, (TOK, TOK), 1)
    allowed = jnp.concatenate(
        [lane - token <= (z - shard_of(z, offset)) * TOK for offset in offsets], axis=1
    )
    flash_heads(q_ref, (keys_ref,), old_state, state, weights_ref, allowed)
    level_ref[...] = rows_of(state[0], diagonal())


def sides(q_ref, left_ref, right_ref, state, level_refs, weights_refs):
    x = position()[0]
    eye = diagonal()

    @pl.when(x > 0)
    def _():
        flash_heads(q_ref, (left_ref,), state, state, weights_refs[0])

    level_refs[0][...] = rows_of(state[0], eye)

    @pl.when(x == NX - 1)
    def _():
        flash_heads(q_ref, (right_ref,), state, state, weights_refs[1])

    level_refs[1][...] = rows_of(state[0], eye)


def first_kernel(q_ref, keys_ref, slot_row_ref, text_ref, *refs):
    state, (level_ref, weights_ref), picked, text_out_ref = refs[:3], refs[3:5], refs[5:8], refs[8]
    text_out_ref[...] = jnp.broadcast_to(text_ref[...].astype(jnp.float32), (8, TOK))
    own_part(NEAR, q_ref, keys_ref, None, state, level_ref, weights_ref)
    pick(slot_row_ref, *picked)


def second_kernel(q_ref, keys_ref, left_ref, right_ref, *refs):
    old_state, state, levels, weights = refs[:3], refs[3:6], refs[6:9], refs[9:]
    own_part(REST, q_ref, keys_ref, old_state, state, levels[0], weights[0])
    sides(q_ref, left_ref, right_ref, state, levels[1:], weights[1:])


def third_kernel(q_ref, left_ref, right_ref, far_0_ref, far_1_ref, *refs):
    old_state, state, levels, weights = refs[:3], refs[3:6], refs[6:9], refs[9:]
    copy_state(old_state, state)
    sides(q_ref, left_ref, right_ref, state, levels, weights)

    @pl.when(position()[0] >= 2)
    def _():
        flash_heads(q_ref, (far_0_ref, far_1_ref), state, state, weights[2])

    levels[2][...] = rows_of(state[0], diagonal())


def pick(slot_row_ref, rows_ref, rest_ref, slots_ref):
    slot_row = slot_row_ref[...]
    slot_col = jnp.transpose(jnp.broadcast_to(slot_row, (TOK, TOK)))
    slots = jnp.where(slot_col >= 0, (slot_col & (KEEP - 1)) + 1, 0)
    slots_ref[...] = slots.astype(jnp.float32).astype(jnp.bfloat16)
    target_row = jnp.where(slot_row >= 0, slot_row >> 5, -1)
    target_col = jnp.where(slot_col >= 0, slot_col >> 5, -1)
    first = lax.broadcasted_iota(jnp.int32, (TOK, TOK), 0)
    second = lax.broadcasted_iota(jnp.int32, (TOK, TOK), 1)
    earlier = jnp.where((target_col == target_row) & (first < second), 1, 0)
    rank = jnp.sum(earlier, axis=0, keepdims=True)
    placed = jnp.where(target_row >= 0, target_row * 2 + rank, -1)[None]
    shape = (SHARDS, 8, TOK)
    to = lax.broadcasted_iota(jnp.int32, shape, 0)
    sub = lax.broadcasted_iota(jnp.int32, shape, 1)
    lane = lax.broadcasted_iota(jnp.int32, shape, 2)

    def one_hot(hit):
        return jnp.where(hit, 1.0, 0.0).reshape(EIGHT, TOK).astype(jnp.bfloat16)

    same = placed == to * 2 + (sub >> 2)
    for h in range(4):
        rows_ref[:, h * TOK : (h + 1) * TOK] = one_hot(same & ((sub & 3) == h))
    rest_ref[:, :TOK] = one_hot((placed == to * 2 + (sub - 2)) & ((sub == 2) | (sub == 3)))
    rest_ref[:, TOK:] = one_hot(lane == jnp.where(sub == 0, to, jnp.where(sub == 1, to + SHARDS, -1)))


def last_kernel(
    q_ref,
    far_2_ref,
    far_3_ref,
    text_ref,
    pick_rows_ref,
    pick_rest_ref,
    slots_ref,
    top_in,
    total_in,
    mixed_in,
    *refs,
):
    levels, weights = refs[:7], refs[7:14]
    context_ref, send_ref, top_ref, total_ref, mixed_ref, weights_last_ref, mass_ref = refs[14:]
    x, z = position()
    old_state = (top_in, total_in, mixed_in)
    state = (top_ref, total_ref, mixed_ref)
    mass_ref[...] = jnp.zeros_like(mass_ref)

    @pl.when(x >= 2)
    def _():
        flash_heads(q_ref, (far_2_ref, far_3_ref), old_state, state, weights_last_ref)

    @pl.when(x < 2)
    def _():
        copy_state(old_state, state)

    context = (mixed_ref[...] / total_ref[...]).astype(jnp.bfloat16)
    for h in range(GROUP):
        context_ref[:, h * HD : (h + 1) * HD] = context[h * TOK : (h + 1) * TOK]

    text = text_ref[...]

    @pl.when(jnp.max(text) > 0.0)
    def _():
        eye = diagonal()
        level = rows_of(top_ref, eye)
        part = text / rows_of(total_ref, eye)

        def mass_of(level_then, weights_ref, at, offsets=NEAR):
            share = jnp.exp2((level_then - level) * FACTOR) * part
            share = jnp.concatenate([share[h : h + 1] for h in range(GROUP)], axis=1)
            high = share.astype(jnp.bfloat16).astype(jnp.float32)
            low = share - high
            both = jnp.concatenate(
                [jnp.broadcast_to(high, (8, ROWS)), jnp.broadcast_to(low, (8, ROWS))], axis=0
            ).astype(jnp.bfloat16)
            added = jnp.dot(both, weights_ref[...], preferred_element_type=jnp.float32)
            added = added[0:1] + added[8:9]
            shift = lax.rem(at, NX) * NZ
            for i, offset in enumerate(offsets):
                to = shift + shard_of(z, offset)
                mass_ref[pl.ds(to, 1), :] = added[:, i * TOK : (i + 1) * TOK]

        own, own_other, left, right, left_other, right_other, far = [
            (level_ref[...], weights_ref) for level_ref, weights_ref in zip(levels, weights)
        ]
        mass_of(*own, x)
        mass_of(*own_other, x, REST)

        @pl.when(x > 0)
        def _():
            mass_of(*left, x + NX - 1)
            mass_of(*left_other, x + NX - 1, REST)

        @pl.when(x == NX - 1)
        def _():
            mass_of(*right, x + 1)
            mass_of(*right_other, x + 1, REST)

        @pl.when(x >= 2)
        def _():
            mass_of(*far, x + 2)
            mass_of(level, weights_last_ref, x + 2, REST)

    half = ROWS // 2
    sides = jnp.concatenate([context[:half], context[half:]], axis=1)
    sides = jnp.dot(pick_rows_ref[...], sides, preferred_element_type=jnp.float32)
    mass = mass_ref[...]
    high = mass.astype(jnp.bfloat16).astype(jnp.float32)
    low = mass - high
    rest = jnp.concatenate([high, low, jnp.zeros((TOK - 2 * SHARDS, HD), jnp.float32)], axis=0)
    rest = jnp.concatenate([slots_ref[...], rest.astype(jnp.bfloat16)], axis=0)
    rest = jnp.dot(pick_rest_ref[...], rest, preferred_element_type=jnp.float32)
    parts = [part.reshape(SHARDS, 8, HD) for part in (sides[:, :HD], sides[:, HD:], rest)]
    send = jnp.concatenate(parts, axis=1).reshape(SEND, HD)
    send_ref[...] = send.astype(jnp.bfloat16)


def place_kernel(got_ref, rows_ref, pay_ref):
    got = got_ref[...].astype(jnp.float32).reshape(SHARDS, SUB, HD)
    mass = jnp.sum(got[:, 16:17, :] + got[:, 17:18, :], axis=0)
    slots = jnp.concatenate(
        [
            jnp.broadcast_to(got[:, 18:19, :], (SHARDS, 4, HD)),
            jnp.broadcast_to(got[:, 19:20, :], (SHARDS, 4, HD)),
        ],
        axis=1,
    ).astype(jnp.int32)
    shape = (SHARDS, 8, HD)
    head = lax.broadcasted_iota(jnp.int32, shape, 1) & 3
    lane = lax.broadcasted_iota(jnp.int32, shape, 2)
    hit = (slots == (lane & (KEEP - 1)) + 1) & (head == lane >> 5)
    put = jnp.where(hit, 1.0, 0.0).reshape(EIGHT, HD).astype(jnp.bfloat16)
    sides = jnp.concatenate(
        [got[:, 0:8].reshape(EIGHT, HD), got[:, 8:16].reshape(EIGHT, HD)], axis=1
    ).astype(jnp.bfloat16)
    rows = lax.dot_general(put, sides, TN, preferred_element_type=jnp.float32)
    rows_ref[...] = rows
    squares = jnp.sum((rows * rows).reshape(4, KEEP, 2 * HD), axis=0)
    squares = jnp.sum(squares, axis=1, keepdims=True)
    squares = row_of(wide(squares), diagonal(KEEP))
    pay = jnp.concatenate([mass, squares, jnp.zeros((6, HD), jnp.float32)], axis=0)
    pay_ref[...] = jnp.broadcast_to(pay[None], (TP, 8, HD))


def finish_kernel(pay_ref, rows_ref, gain_ref, text_ref, mass_ref, kept_ref):
    pay = jnp.sum(pay_ref[...], axis=0)
    mass_ref[...] = pay[0:1] * (1.0 - text_ref[...].astype(jnp.float32))
    squares = jnp.where(diagonal(KEEP), jnp.broadcast_to(pay[1:2], (KEEP, HD)), 0.0)
    factor = lax.rsqrt(wide(jnp.sum(squares, axis=1, keepdims=True)) / D + 1e-06)
    for h in range(GROUP):
        columns = slice(h * HD, (h + 1) * HD)
        rows = slice((h & 3) * KEEP, ((h & 3) + 1) * KEEP)
        side = slice((h >> 2) * HD, ((h >> 2) + 1) * HD)
        kept_ref[:, columns] = (rows_ref[rows, side] * factor * gain_ref[:, columns]).astype(
            jnp.bfloat16
        )


def shape_of(shape, dtype):
    return jax.ShapeDtypeStruct(shape, dtype)


def shifted(value, axis, step, count):
    return lax.ppermute(value, axis, [(i, (i + step) % count) for i in range(count)])


def cost(flops):
    return pl.CostEstimate(flops=flops, bytes_accessed=2**10, transcendentals=0)


def on_device(queries, key_rows, value_rows, text_mask, kept_slot, norm_gain):
    f32, bf16 = jnp.float32, jnp.bfloat16
    both = jnp.stack([key_rows, value_rows])
    over_z = ("zh", "zl")
    same = jnp.stack([both] + [shifted(both, over_z, step, NZ) for step in (2, -2, 4)])
    other = shifted(same, over_z, -1, NZ)
    state = [shape_of((ROWS, HD), f32)] * 3
    level = shape_of((GROUP, TOK), f32)
    near_weights = shape_of((ROWS, len(NEAR) * TOK), bf16)
    rest_weights = shape_of((ROWS, len(REST) * TOK), bf16)

    def kernel(body, name, inputs, out_shape, scratch=()):
        return pl.pallas_call(
            body,
            in_specs=[vmem()] * len(inputs),
            out_specs=[vmem()] * len(out_shape),
            out_shape=out_shape,
            scratch_shapes=list(scratch),
            compiler_params=params(),
            cost_estimate=cost(10**9),
            name=name,
        )(*inputs)

    *now, level_own, weights_own, pick_rows, pick_rest, slots, text = kernel(
        first_kernel,
        "first",
        [queries, same, kept_slot[None], text_mask[None]],
        state
        + [level, near_weights]
        + [shape_of((EIGHT, 4 * TOK), bf16), shape_of((EIGHT, 2 * TOK), bf16)]
        + [shape_of((TOK, HD), bf16), shape_of((8, TOK), f32)],
    )
    other, now[0] = lax.optimization_barrier((other, now[0]))
    left = [shifted(part, "x", 1, NX) for part in (same, other)]
    right = [shifted(part, "x", -1, NX) for part in (same, other)]
    outs = kernel(
        second_kernel,
        "second",
        [queries, other, left[0], right[0], *now],
        state + [level] * 3 + [rest_weights, near_weights, near_weights],
    )
    now, levels, kept = list(outs[:3]), [level_own, *outs[3:6]], [weights_own, *outs[6:]]
    left[1], right[1], now[0] = lax.optimization_barrier((left[1], right[1], now[0]))
    half = 2
    far = []
    for i in range(2):
        far.append(shifted(left[i][:half], "x", 1, NX))
        far.append(shifted(right[i][half:], "x", -1, NX))
    outs = kernel(
        third_kernel,
        "third",
        [queries, left[1], right[1], *far[:2], *now],
        state + [level] * 3 + [rest_weights, rest_weights, near_weights],
    )
    now, levels, kept = outs[:3], [*levels, *outs[3:6]], [*kept, *outs[6:]]
    context, send = kernel(
        last_kernel,
        "last",
        [queries, *far[2:], text, pick_rows, pick_rest, slots, *now, *levels, *kept],
        [shape_of((TOK, GROUP * HD), bf16), shape_of((SEND, HD), bf16)],
        [pltpu.VMEM((ROWS, HD), f32)] * 3
        + [pltpu.VMEM((ROWS, len(REST) * TOK), bf16), pltpu.VMEM((SHARDS, HD), f32)],
    )
    got = lax.all_to_all(
        send.reshape(SHARDS, SUB, HD), ("x", "zh", "zl"), split_axis=0, concat_axis=0, tiled=True
    ).reshape(SEND, HD)
    rows, pay = pl.pallas_call(
        place_kernel,
        in_specs=[vmem()],
        out_specs=[vmem()] * 2,
        out_shape=[shape_of((4 * KEEP, 2 * HD), f32), shape_of((TP, 8, HD), f32)],
        compiler_params=params(),
        name="place_rows",
    )(got)
    pay = lax.all_to_all(pay, ("y", "core"), split_axis=0, concat_axis=0, tiled=True)
    mass, kept = pl.pallas_call(
        finish_kernel,
        in_specs=[vmem()] * 4,
        out_specs=[vmem()] * 2,
        out_shape=[shape_of((1, TOK), f32), shape_of((KEEP, GROUP * HD), bf16)],
        compiler_params=params(),
        name="finish",
    )(pay, rows, norm_gain[None], text_mask[None])
    return context, mass[0], kept


def solution(mesh):
    cut = Mesh(mesh.devices.reshape(NX, NZ // 2, 2, 4, 2), ("x", "zh", "zl", "y", "core"))
    seq, tp = ("x", "zh", "zl"), ("y", "core")
    placed = (P(seq, tp), P(seq, tp), P(seq, tp), P(seq), P(seq), P(tp))
    return jax.shard_map(
        on_device,
        mesh=cut,
        in_specs=placed,
        out_specs=(P(seq, tp), P(seq), P(seq, tp)),
        check_vma=False,
    )
```

```python
import math

import jax
import jax.numpy as jnp
from jax import lax
from jax.experimental import pallas as pl
from jax.experimental.pallas import tpu as pltpu
from jax.sharding import Mesh, PartitionSpec as P

HD = 128
D = 8192
TOK = 128
GROUP = 8
ROWS = GROUP * TOK
NX = 4
NZ = 8
SHARDS = NX * NZ
KEEP = 32
SUB = 24
SEND = SHARDS * SUB
EIGHT = SHARDS * 8
TP = 8
NEAR = (0, 4, -2, 2)
REST = (1, 5, -1, 3)
FACTOR = math.log2(math.e) / math.sqrt(HD)
LOW = -1e30
NT = (((1,), (1,)), ((), ()))
TN = (((0,), (0,)), ((), ()))
VMEM_BYTES = 40 * 1024 * 1024


def vmem():
    return pl.BlockSpec(memory_space=pltpu.VMEM)


def params():
    return pltpu.CompilerParams(vmem_limit_bytes=VMEM_BYTES)


def wide(column):
    return jnp.broadcast_to(column, (column.shape[0], 128))


def tiled(array, count):
    return jnp.concatenate([array] * count, axis=1)


def position():
    return lax.axis_index("x"), lax.axis_index("zh") * 2 + lax.axis_index("zl")


def diagonal(rows=TOK):
    return lax.broadcasted_iota(jnp.int32, (rows, TOK), 0) == lax.broadcasted_iota(
        jnp.int32, (rows, TOK), 1
    )


def row_of(column, eye):
    return jnp.sum(jnp.where(eye, column, 0.0), axis=0, keepdims=True)


def rows_of(ref, eye):
    return jnp.concatenate(
        [row_of(ref[h * TOK : (h + 1) * TOK], eye) for h in range(GROUP)], axis=0
    )


def keys_of(*refs):
    return jnp.concatenate([ref[:, 0].reshape(-1, HD) for ref in refs], axis=0)


def values_of(*refs):
    value = jnp.concatenate([ref[:, 1].reshape(-1, HD) for ref in refs], axis=0)
    return jnp.concatenate([value, jnp.ones_like(value)], axis=1)


def shard_of(z, offset):
    return (z + offset) & (NZ - 1)


def flash(query, key, value, old, weights_ref, rows, allowed=None):
    count = key.shape[0] // TOK
    scores = lax.dot_general(query, key, NT, preferred_element_type=jnp.float32)
    if allowed is not None:
        scores = jnp.where(allowed, scores, LOW)
    best = scores[:, 0:TOK]
    for i in range(1, count):
        best = jnp.maximum(best, scores[:, i * TOK : (i + 1) * TOK])
    top = wide(jnp.max(best, axis=1, keepdims=True))
    if old is not None:
        top = jnp.maximum(old[0], top)
    weights = jnp.exp2((scores - tiled(top, count)) * FACTOR).astype(jnp.bfloat16)
    weights_ref[rows] = weights
    both = jnp.dot(weights, value, preferred_element_type=jnp.float32)
    mixed, total = both[:, :HD], both[:, HD:]
    if old is not None:
        shrink = jnp.exp2((old[0] - top) * FACTOR)
        total = total + old[1] * shrink
        mixed = mixed + old[2] * shrink
    return top, total, mixed


def flash_heads(q_ref, pair, old_state, state, weights_ref, allowed=None):
    key = keys_of(*pair)
    value = values_of(*pair)
    for h in range(GROUP):
        rows = slice(h * TOK, (h + 1) * TOK)
        query = q_ref[:, h * HD : (h + 1) * HD]
        old = None if old_state is None else tuple(ref[rows] for ref in old_state)
        for ref, part in zip(state, flash(query, key, value, old, weights_ref, rows, allowed)):
            ref[rows] = part


def copy_state(old_state, state):
    for ref, old in zip(state, old_state):
        ref[...] = old[...]


def own_part(offsets, q_ref, keys_ref, old_state, state, level_ref, weights_ref):
    z = position()[1]
    token = lax.broadcasted_iota(jnp.int32, (TOK, TOK), 0)
    lane = lax.broadcasted_iota(jnp.int32, (TOK, TOK), 1)
    allowed = jnp.concatenate(
        [lane - token <= (z - shard_of(z, offset)) * TOK for offset in offsets], axis=1
    )
    flash_heads(q_ref, (keys_ref,), old_state, state, weights_ref, allowed)
    level_ref[...] = rows_of(state[0], diagonal())


def sides(q_ref, left_ref, right_ref, state, level_refs, weights_refs):
    x = position()[0]
    eye = diagonal()

    @pl.when(x > 0)
    def _():
        flash_heads(q_ref, (left_ref,), state, state, weights_refs[0])

    level_refs[0][...] = rows_of(state[0], eye)

    @pl.when(x == NX - 1)
    def _():
        flash_heads(q_ref, (right_ref,), state, state, weights_refs[1])

    level_refs[1][...] = rows_of(state[0], eye)


def first_kernel(q_ref, keys_ref, slot_row_ref, text_ref, *refs):
    state, (level_ref, weights_ref), picked, text_out_ref = refs[:3], refs[3:5], refs[5:8], refs[8]
    text_out_ref[...] = jnp.broadcast_to(text_ref[...].astype(jnp.float32), (8, TOK))
    own_part(NEAR, q_ref, keys_ref, None, state, level_ref, weights_ref)
    pick(slot_row_ref, *picked)


def second_kernel(q_ref, keys_ref, left_ref, right_ref, *refs):
    old_state, state, levels, weights = refs[:3], refs[3:6], refs[6:9], refs[9:]
    own_part(REST, q_ref, keys_ref, old_state, state, levels[0], weights[0])
    sides(q_ref, left_ref, right_ref, state, levels[1:], weights[1:])


def third_kernel(q_ref, left_ref, right_ref, far_0_ref, far_1_ref, *refs):
    old_state, state, levels, weights = refs[:3], refs[3:6], refs[6:9], refs[9:]
    copy_state(old_state, state)
    sides(q_ref, left_ref, right_ref, state, levels, weights)

    @pl.when(position()[0] >= 2)
    def _():
        flash_heads(q_ref, (far_0_ref, far_1_ref), state, state, weights[2])

    levels[2][...] = rows_of(state[0], diagonal())


def pick(slot_row_ref, rows_ref, rest_ref, slots_ref):
    slot_row = slot_row_ref[...]
    slot_col = jnp.transpose(jnp.broadcast_to(slot_row, (TOK, TOK)))
    slots = jnp.where(slot_col >= 0, (slot_col & (KEEP - 1)) + 1, 0)
    slots_ref[...] = slots.astype(jnp.float32).astype(jnp.bfloat16)
    target_row = jnp.where(slot_row >= 0, slot_row >> 5, -1)
    target_col = jnp.where(slot_col >= 0, slot_col >> 5, -1)
    first = lax.broadcasted_iota(jnp.int32, (TOK, TOK), 0)
    second = lax.broadcasted_iota(jnp.int32, (TOK, TOK), 1)
    earlier = jnp.where((target_col == target_row) & (first < second), 1, 0)
    rank = jnp.sum(earlier, axis=0, keepdims=True)
    placed = jnp.where(target_row >= 0, target_row * 2 + rank, -1)[None]
    shape = (SHARDS, 8, TOK)
    to = lax.broadcasted_iota(jnp.int32, shape, 0)
    sub = lax.broadcasted_iota(jnp.int32, shape, 1)
    lane = lax.broadcasted_iota(jnp.int32, shape, 2)

    def one_hot(hit):
        return jnp.where(hit, 1.0, 0.0).reshape(EIGHT, TOK).astype(jnp.bfloat16)

    same = placed == to * 2 + (sub >> 2)
    for h in range(4):
        rows_ref[:, h * TOK : (h + 1) * TOK] = one_hot(same & ((sub & 3) == h))
    rest_ref[:, :TOK] = one_hot((placed == to * 2 + (sub - 2)) & ((sub == 2) | (sub == 3)))
    rest_ref[:, TOK:] = one_hot(lane == jnp.where(sub == 0, to, jnp.where(sub == 1, to + SHARDS, -1)))


def last_kernel(
    q_ref,
    far_2_ref,
    far_3_ref,
    text_ref,
    pick_rows_ref,
    pick_rest_ref,
    slots_ref,
    top_in,
    total_in,
    mixed_in,
    *refs,
):
    levels, weights = refs[:7], refs[7:14]
    context_ref, send_ref, top_ref, total_ref, mixed_ref, weights_last_ref, mass_ref = refs[14:]
    x, z = position()
    old_state = (top_in, total_in, mixed_in)
    state = (top_ref, total_ref, mixed_ref)
    mass_ref[...] = jnp.zeros_like(mass_ref)

    @pl.when(x >= 2)
    def _():
        flash_heads(q_ref, (far_2_ref, far_3_ref), old_state, state, weights_last_ref)

    @pl.when(x < 2)
    def _():
        copy_state(old_state, state)

    context = (mixed_ref[...] / total_ref[...]).astype(jnp.bfloat16)
    for h in range(GROUP):
        context_ref[:, h * HD : (h + 1) * HD] = context[h * TOK : (h + 1) * TOK]

    text = text_ref[...]

    @pl.when(jnp.max(text) > 0.0)
    def _():
        eye = diagonal()
        level = rows_of(top_ref, eye)
        part = text / rows_of(total_ref, eye)

        def mass_of(level_then, weights_ref, at, offsets=NEAR):
            share = jnp.exp2((level_then - level) * FACTOR) * part
            share = jnp.concatenate([share[h : h + 1] for h in range(GROUP)], axis=1)
            high = share.astype(jnp.bfloat16).astype(jnp.float32)
            low = share - high
            both = jnp.concatenate(
                [jnp.broadcast_to(high, (8, ROWS)), jnp.broadcast_to(low, (8, ROWS))], axis=0
            ).astype(jnp.bfloat16)
            added = jnp.dot(both, weights_ref[...], preferred_element_type=jnp.float32)
            added = added[0:1] + added[8:9]
            shift = lax.rem(at, NX) * NZ
            for i, offset in enumerate(offsets):
                to = shift + shard_of(z, offset)
                mass_ref[pl.ds(to, 1), :] = added[:, i * TOK : (i + 1) * TOK]

        own, own_other, left, right, left_other, right_other, far = [
            (level_ref[...], weights_ref) for level_ref, weights_ref in zip(levels, weights)
        ]
        mass_of(*own, x)
        mass_of(*own_other, x, REST)

        @pl.when(x > 0)
        def _():
            mass_of(*left, x + NX - 1)
            mass_of(*left_other, x + NX - 1, REST)

        @pl.when(x == NX - 1)
        def _():
            mass_of(*right, x + 1)
            mass_of(*right_other, x + 1, REST)

        @pl.when(x >= 2)
        def _():
            mass_of(*far, x + 2)
            mass_of(level, weights_last_ref, x + 2, REST)

    half = ROWS // 2
    sides = jnp.concatenate([context[:half], context[half:]], axis=1)
    sides = jnp.dot(pick_rows_ref[...], sides, preferred_element_type=jnp.float32)
    mass = mass_ref[...]
    high = mass.astype(jnp.bfloat16).astype(jnp.float32)
    low = mass - high
    rest = jnp.concatenate([high, low, jnp.zeros((TOK - 2 * SHARDS, HD), jnp.float32)], axis=0)
    rest = jnp.concatenate([slots_ref[...], rest.astype(jnp.bfloat16)], axis=0)
    rest = jnp.dot(pick_rest_ref[...], rest, preferred_element_type=jnp.float32)
    parts = [part.reshape(SHARDS, 8, HD) for part in (sides[:, :HD], sides[:, HD:], rest)]
    send = jnp.concatenate(parts, axis=1).reshape(SEND, HD)
    send_ref[...] = send.astype(jnp.bfloat16)


def place_kernel(got_ref, rows_ref, pay_ref):
    got = got_ref[...].astype(jnp.float32).reshape(SHARDS, SUB, HD)
    mass = jnp.sum(got[:, 16:17, :] + got[:, 17:18, :], axis=0)
    slots = jnp.concatenate(
        [
            jnp.broadcast_to(got[:, 18:19, :], (SHARDS, 4, HD)),
            jnp.broadcast_to(got[:, 19:20, :], (SHARDS, 4, HD)),
        ],
        axis=1,
    ).astype(jnp.int32)
    shape = (SHARDS, 8, HD)
    head = lax.broadcasted_iota(jnp.int32, shape, 1) & 3
    lane = lax.broadcasted_iota(jnp.int32, shape, 2)
    hit = (slots == (lane & (KEEP - 1)) + 1) & (head == lane >> 5)
    put = jnp.where(hit, 1.0, 0.0).reshape(EIGHT, HD).astype(jnp.bfloat16)
    sides = jnp.concatenate(
        [got[:, 0:8].reshape(EIGHT, HD), got[:, 8:16].reshape(EIGHT, HD)], axis=1
    ).astype(jnp.bfloat16)
    rows = lax.dot_general(put, sides, TN, preferred_element_type=jnp.float32)
    rows_ref[...] = rows
    squares = jnp.sum((rows * rows).reshape(4, KEEP, 2 * HD), axis=0)
    squares = jnp.sum(squares, axis=1, keepdims=True)
    squares = row_of(wide(squares), diagonal(KEEP))
    pay = jnp.concatenate([mass, squares, jnp.zeros((6, HD), jnp.float32)], axis=0)
    pay_ref[...] = jnp.broadcast_to(pay[None], (TP, 8, HD))


def finish_kernel(pay_ref, rows_ref, gain_ref, text_ref, mass_ref, kept_ref):
    pay = jnp.sum(pay_ref[...], axis=0)
    mass_ref[...] = pay[0:1] * (1.0 - text_ref[...].astype(jnp.float32))
    squares = jnp.where(diagonal(KEEP), jnp.broadcast_to(pay[1:2], (KEEP, HD)), 0.0)
    factor = lax.rsqrt(wide(jnp.sum(squares, axis=1, keepdims=True)) / D + 1e-06)
    for h in range(GROUP):
        columns = slice(h * HD, (h + 1) * HD)
        rows = slice((h & 3) * KEEP, ((h & 3) + 1) * KEEP)
        side = slice((h >> 2) * HD, ((h >> 2) + 1) * HD)
        kept_ref[:, columns] = (rows_ref[rows, side] * factor * gain_ref[:, columns]).astype(
            jnp.bfloat16
        )


def shape_of(shape, dtype):
    return jax.ShapeDtypeStruct(shape, dtype)


def shifted(value, axis, step, count):
    return lax.ppermute(value, axis, [(i, (i + step) % count) for i in range(count)])


def cost(flops):
    return pl.CostEstimate(flops=flops, bytes_accessed=2**10, transcendentals=0)


def on_device(queries, key_rows, value_rows, text_mask, kept_slot, norm_gain):
    f32, bf16 = jnp.float32, jnp.bfloat16
    both = jnp.stack([key_rows, value_rows])
    over_z = ("zh", "zl")
    same = jnp.stack([both] + [shifted(both, over_z, step, NZ) for step in (4, 2, -2)])
    other = shifted(same, over_z, -1, NZ)
    state = [shape_of((ROWS, HD), f32)] * 3
    level = shape_of((GROUP, TOK), f32)
    near_weights = shape_of((ROWS, len(NEAR) * TOK), bf16)
    rest_weights = shape_of((ROWS, len(REST) * TOK), bf16)

    def kernel(body, name, inputs, out_shape, scratch=()):
        return pl.pallas_call(
            body,
            in_specs=[vmem()] * len(inputs),
            out_specs=[vmem()] * len(out_shape),
            out_shape=out_shape,
            scratch_shapes=list(scratch),
            compiler_params=params(),
            cost_estimate=cost(10**9),
            name=name,
        )(*inputs)

    *now, level_own, weights_own, pick_rows, pick_rest, slots, text = kernel(
        first_kernel,
        "first",
        [queries, same, kept_slot[None], text_mask[None]],
        state
        + [level, near_weights]
        + [shape_of((EIGHT, 4 * TOK), bf16), shape_of((EIGHT, 2 * TOK), bf16)]
        + [shape_of((TOK, HD), bf16), shape_of((8, TOK), f32)],
    )
    other, now[0] = lax.optimization_barrier((other, now[0]))
    left = [shifted(part, "x", 1, NX) for part in (same, other)]
    right = [shifted(part, "x", -1, NX) for part in (same, other)]
    outs = kernel(
        second_kernel,
        "second",
        [queries, other, left[0], right[0], *now],
        state + [level] * 3 + [rest_weights, near_weights, near_weights],
    )
    now, levels, kept = list(outs[:3]), [level_own, *outs[3:6]], [weights_own, *outs[6:]]
    left[1], right[1], now[0] = lax.optimization_barrier((left[1], right[1], now[0]))
    half = 2
    far = []
    for i in range(2):
        far.append(shifted(left[i][:half], "x", 1, NX))
        far.append(shifted(right[i][half:], "x", -1, NX))
    outs = kernel(
        third_kernel,
        "third",
        [queries, left[1], right[1], *far[:2], *now],
        state + [level] * 3 + [rest_weights, rest_weights, near_weights],
    )
    now, levels, kept = outs[:3], [*levels, *outs[3:6]], [*kept, *outs[6:]]
    context, send = kernel(
        last_kernel,
        "last",
        [queries, *far[2:], text, pick_rows, pick_rest, slots, *now, *levels, *kept],
        [shape_of((TOK, GROUP * HD), bf16), shape_of((SEND, HD), bf16)],
        [pltpu.VMEM((ROWS, HD), f32)] * 3
        + [pltpu.VMEM((ROWS, len(REST) * TOK), bf16), pltpu.VMEM((SHARDS, HD), f32)],
    )
    got = lax.all_to_all(
        send.reshape(SHARDS, SUB, HD), ("x", "zh", "zl"), split_axis=0, concat_axis=0, tiled=True
    ).reshape(SEND, HD)
    rows, pay = pl.pallas_call(
        place_kernel,
        in_specs=[vmem()],
        out_specs=[vmem()] * 2,
        out_shape=[shape_of((4 * KEEP, 2 * HD), f32), shape_of((TP, 8, HD), f32)],
        compiler_params=params(),
        name="place_rows",
    )(got)
    pay = lax.all_to_all(pay, ("y", "core"), split_axis=0, concat_axis=0, tiled=True)
    mass, kept = pl.pallas_call(
        finish_kernel,
        in_specs=[vmem()] * 4,
        out_specs=[vmem()] * 2,
        out_shape=[shape_of((1, TOK), f32), shape_of((KEEP, GROUP * HD), bf16)],
        compiler_params=params(),
        name="finish",
    )(pay, rows, norm_gain[None], text_mask[None])
    return context, mass[0], kept


def solution(mesh):
    cut = Mesh(mesh.devices.reshape(NX, NZ // 2, 2, 4, 2), ("x", "zh", "zl", "y", "core"))
    seq, tp = ("x", "zh", "zl"), ("y", "core")
    placed = (P(seq, tp), P(seq, tp), P(seq, tp), P(seq), P(seq), P(tp))
    return jax.shard_map(
        on_device,
        mesh=cut,
        in_specs=placed,
        out_specs=(P(seq, tp), P(seq), P(seq, tp)),
        check_vma=False,
    )
```

```python
import math

import jax
import jax.numpy as jnp
from jax import lax
from jax.experimental import pallas as pl
from jax.experimental.pallas import tpu as pltpu
from jax.sharding import Mesh, PartitionSpec as P

HD = 128
D = 8192
TOK = 128
GROUP = 8
ROWS = GROUP * TOK
NX = 4
NZ = 8
SHARDS = NX * NZ
KEEP = 32
SUB = 24
SEND = SHARDS * SUB
EIGHT = SHARDS * 8
TP = 8
NEAR = (0, 4, -2, 2)
REST = (1, 5, -1, 3)
FACTOR = math.log2(math.e) / math.sqrt(HD)
LOW = -1e30
TO_RIGHT = [(0, 1), (1, 2), (2, 3)]
TO_LEFT = [(0, 3), (1, 0)]
FAR_RIGHT = [(1, 2), (2, 3)]
FAR_LEFT = [(0, 3), (3, 2)]
NT = (((1,), (1,)), ((), ()))
TN = (((0,), (0,)), ((), ()))
VMEM_BYTES = 40 * 1024 * 1024


def vmem():
    return pl.BlockSpec(memory_space=pltpu.VMEM)


def params():
    return pltpu.CompilerParams(vmem_limit_bytes=VMEM_BYTES)


def wide(column):
    return jnp.broadcast_to(column, (column.shape[0], 128))


def tiled(array, count):
    return jnp.concatenate([array] * count, axis=1)


def position():
    return lax.axis_index("x"), lax.axis_index("zh") * 2 + lax.axis_index("zl")


def diagonal(rows=TOK):
    return lax.broadcasted_iota(jnp.int32, (rows, TOK), 0) == lax.broadcasted_iota(
        jnp.int32, (rows, TOK), 1
    )


def row_of(column, eye):
    return jnp.sum(jnp.where(eye, column, 0.0), axis=0, keepdims=True)


def rows_of(ref, eye):
    return jnp.concatenate(
        [row_of(ref[h * TOK : (h + 1) * TOK], eye) for h in range(GROUP)], axis=0
    )


def keys_of(*refs):
    return jnp.concatenate([ref[:, 0].reshape(-1, HD) for ref in refs], axis=0)


def values_of(*refs):
    value = jnp.concatenate([ref[:, 1].reshape(-1, HD) for ref in refs], axis=0)
    return jnp.concatenate([value, jnp.ones_like(value)], axis=1)


def shard_of(z, offset):
    return (z + offset) & (NZ - 1)


def flash(query, key, value, old, weights_ref, rows, allowed=None):
    count = key.shape[0] // TOK
    scores = lax.dot_general(query, key, NT, preferred_element_type=jnp.float32)
    if allowed is not None:
        scores = jnp.where(allowed, scores, LOW)
    best = scores[:, 0:TOK]
    for i in range(1, count):
        best = jnp.maximum(best, scores[:, i * TOK : (i + 1) * TOK])
    top = wide(jnp.max(best, axis=1, keepdims=True))
    if old is not None:
        top = jnp.maximum(old[0], top)
    weights = jnp.exp2((scores - tiled(top, count)) * FACTOR).astype(jnp.bfloat16)
    weights_ref[rows] = weights
    both = jnp.dot(weights, value, preferred_element_type=jnp.float32)
    mixed, total = both[:, :HD], both[:, HD:]
    if old is not None:
        shrink = jnp.exp2((old[0] - top) * FACTOR)
        total = total + old[1] * shrink
        mixed = mixed + old[2] * shrink
    return top, total, mixed


def flash_heads(q_ref, pair, old_state, state, weights_ref, allowed=None):
    key = keys_of(*pair)
    value = values_of(*pair)
    for h in range(GROUP):
        rows = slice(h * TOK, (h + 1) * TOK)
        query = q_ref[:, h * HD : (h + 1) * HD]
        old = None if old_state is None else tuple(ref[rows] for ref in old_state)
        for ref, part in zip(state, flash(query, key, value, old, weights_ref, rows, allowed)):
            ref[rows] = part


def copy_state(old_state, state):
    for ref, old in zip(state, old_state):
        ref[...] = old[...]


def own_part(offsets, q_ref, keys_ref, old_state, state, level_ref, weights_ref):
    z = position()[1]
    token = lax.broadcasted_iota(jnp.int32, (TOK, TOK), 0)
    lane = lax.broadcasted_iota(jnp.int32, (TOK, TOK), 1)
    allowed = jnp.concatenate(
        [lane - token <= (z - shard_of(z, offset)) * TOK for offset in offsets], axis=1
    )
    flash_heads(q_ref, (keys_ref,), old_state, state, weights_ref, allowed)
    level_ref[...] = rows_of(state[0], diagonal())


def sides(q_ref, left_ref, right_ref, state, level_refs, weights_refs):
    x = position()[0]
    eye = diagonal()

    @pl.when(x > 0)
    def _():
        flash_heads(q_ref, (left_ref,), state, state, weights_refs[0])

    level_refs[0][...] = rows_of(state[0], eye)

    @pl.when(x == NX - 1)
    def _():
        flash_heads(q_ref, (right_ref,), state, state, weights_refs[1])

    level_refs[1][...] = rows_of(state[0], eye)


def first_kernel(q_ref, keys_ref, slot_row_ref, text_ref, *refs):
    state, (level_ref, weights_ref), picked, text_out_ref = refs[:3], refs[3:5], refs[5:8], refs[8]
    text_out_ref[...] = jnp.broadcast_to(text_ref[...].astype(jnp.float32), (8, TOK))
    own_part(NEAR, q_ref, keys_ref, None, state, level_ref, weights_ref)
    pick(slot_row_ref, *picked)


def second_kernel(q_ref, keys_ref, left_ref, right_ref, *refs):
    old_state, state, levels, weights = refs[:3], refs[3:6], refs[6:9], refs[9:]
    own_part(REST, q_ref, keys_ref, old_state, state, levels[0], weights[0])
    sides(q_ref, left_ref, right_ref, state, levels[1:], weights[1:])


def third_kernel(q_ref, left_ref, right_ref, far_0_ref, far_1_ref, *refs):
    old_state, state, levels, weights = refs[:3], refs[3:6], refs[6:9], refs[9:]
    copy_state(old_state, state)
    sides(q_ref, left_ref, right_ref, state, levels, weights)

    @pl.when(position()[0] >= 2)
    def _():
        flash_heads(q_ref, (far_0_ref, far_1_ref), state, state, weights[2])

    levels[2][...] = rows_of(state[0], diagonal())


def pick(slot_row_ref, rows_ref, rest_ref, slots_ref):
    slot_row = slot_row_ref[...]
    slot_col = jnp.transpose(jnp.broadcast_to(slot_row, (TOK, TOK)))
    slots = jnp.where(slot_col >= 0, (slot_col & (KEEP - 1)) + 1, 0)
    slots_ref[...] = slots.astype(jnp.float32).astype(jnp.bfloat16)
    target_row = jnp.where(slot_row >= 0, slot_row >> 5, -1)
    target_col = jnp.where(slot_col >= 0, slot_col >> 5, -1)
    first = lax.broadcasted_iota(jnp.int32, (TOK, TOK), 0)
    second = lax.broadcasted_iota(jnp.int32, (TOK, TOK), 1)
    earlier = jnp.where((target_col == target_row) & (first < second), 1, 0)
    rank = jnp.sum(earlier, axis=0, keepdims=True)
    placed = jnp.where(target_row >= 0, target_row * 2 + rank, -1)[None]
    shape = (SHARDS, 8, TOK)
    to = lax.broadcasted_iota(jnp.int32, shape, 0)
    sub = lax.broadcasted_iota(jnp.int32, shape, 1)
    lane = lax.broadcasted_iota(jnp.int32, shape, 2)

    def one_hot(hit):
        return jnp.where(hit, 1.0, 0.0).reshape(EIGHT, TOK).astype(jnp.bfloat16)

    same = placed == to * 2 + (sub >> 2)
    for h in range(4):
        rows_ref[:, h * TOK : (h + 1) * TOK] = one_hot(same & ((sub & 3) == h))
    rest_ref[:, :TOK] = one_hot((placed == to * 2 + (sub - 2)) & ((sub == 2) | (sub == 3)))
    rest_ref[:, TOK:] = one_hot(lane == jnp.where(sub == 0, to, jnp.where(sub == 1, to + SHARDS, -1)))


def last_kernel(
    q_ref,
    far_2_ref,
    far_3_ref,
    text_ref,
    pick_rows_ref,
    pick_rest_ref,
    slots_ref,
    top_in,
    total_in,
    mixed_in,
    *refs,
):
    levels, weights = refs[:7], refs[7:14]
    context_ref, send_ref, top_ref, total_ref, mixed_ref, weights_last_ref, mass_ref = refs[14:]
    x, z = position()
    old_state = (top_in, total_in, mixed_in)
    state = (top_ref, total_ref, mixed_ref)
    mass_ref[...] = jnp.zeros_like(mass_ref)

    @pl.when(x >= 2)
    def _():
        flash_heads(q_ref, (far_2_ref, far_3_ref), old_state, state, weights_last_ref)

    @pl.when(x < 2)
    def _():
        copy_state(old_state, state)

    context = (mixed_ref[...] / total_ref[...]).astype(jnp.bfloat16)
    for h in range(GROUP):
        context_ref[:, h * HD : (h + 1) * HD] = context[h * TOK : (h + 1) * TOK]

    text = text_ref[...]

    @pl.when(jnp.max(text) > 0.0)
    def _():
        eye = diagonal()
        level = rows_of(top_ref, eye)
        part = text / rows_of(total_ref, eye)

        def mass_of(level_then, weights_ref, at, offsets=NEAR):
            share = jnp.exp2((level_then - level) * FACTOR) * part
            share = jnp.concatenate([share[h : h + 1] for h in range(GROUP)], axis=1)
            high = share.astype(jnp.bfloat16).astype(jnp.float32)
            low = share - high
            both = jnp.concatenate(
                [jnp.broadcast_to(high, (8, ROWS)), jnp.broadcast_to(low, (8, ROWS))], axis=0
            ).astype(jnp.bfloat16)
            added = jnp.dot(both, weights_ref[...], preferred_element_type=jnp.float32)
            added = added[0:1] + added[8:9]
            shift = lax.rem(at, NX) * NZ
            for i, offset in enumerate(offsets):
                to = shift + shard_of(z, offset)
                mass_ref[pl.ds(to, 1), :] = added[:, i * TOK : (i + 1) * TOK]

        own, own_other, left, right, left_other, right_other, far = [
            (level_ref[...], weights_ref) for level_ref, weights_ref in zip(levels, weights)
        ]
        mass_of(*own, x)
        mass_of(*own_other, x, REST)

        @pl.when(x > 0)
        def _():
            mass_of(*left, x + NX - 1)
            mass_of(*left_other, x + NX - 1, REST)

        @pl.when(x == NX - 1)
        def _():
            mass_of(*right, x + 1)
            mass_of(*right_other, x + 1, REST)

        @pl.when(x >= 2)
        def _():
            mass_of(*far, x + 2)
            mass_of(level, weights_last_ref, x + 2, REST)

    half = ROWS // 2
    sides = jnp.concatenate([context[:half], context[half:]], axis=1)
    sides = jnp.dot(pick_rows_ref[...], sides, preferred_element_type=jnp.float32)
    mass = mass_ref[...]
    high = mass.astype(jnp.bfloat16).astype(jnp.float32)
    low = mass - high
    rest = jnp.concatenate([high, low, jnp.zeros((TOK - 2 * SHARDS, HD), jnp.float32)], axis=0)
    rest = jnp.concatenate([slots_ref[...], rest.astype(jnp.bfloat16)], axis=0)
    rest = jnp.dot(pick_rest_ref[...], rest, preferred_element_type=jnp.float32)
    parts = [part.reshape(SHARDS, 8, HD) for part in (sides[:, :HD], sides[:, HD:], rest)]
    send = jnp.concatenate(parts, axis=1).reshape(SEND, HD)
    send_ref[...] = send.astype(jnp.bfloat16)


def place_kernel(got_ref, rows_ref, pay_ref):
    got = got_ref[...].astype(jnp.float32).reshape(SHARDS, SUB, HD)
    mass = jnp.sum(got[:, 16:17, :] + got[:, 17:18, :], axis=0)
    slots = jnp.concatenate(
        [
            jnp.broadcast_to(got[:, 18:19, :], (SHARDS, 4, HD)),
            jnp.broadcast_to(got[:, 19:20, :], (SHARDS, 4, HD)),
        ],
        axis=1,
    ).astype(jnp.int32)
    shape = (SHARDS, 8, HD)
    head = lax.broadcasted_iota(jnp.int32, shape, 1) & 3
    lane = lax.broadcasted_iota(jnp.int32, shape, 2)
    hit = (slots == (lane & (KEEP - 1)) + 1) & (head == lane >> 5)
    put = jnp.where(hit, 1.0, 0.0).reshape(EIGHT, HD).astype(jnp.bfloat16)
    sides = jnp.concatenate(
        [got[:, 0:8].reshape(EIGHT, HD), got[:, 8:16].reshape(EIGHT, HD)], axis=1
    ).astype(jnp.bfloat16)
    rows = lax.dot_general(put, sides, TN, preferred_element_type=jnp.float32)
    rows_ref[...] = rows
    squares = jnp.sum((rows * rows).reshape(4, KEEP, 2 * HD), axis=0)
    squares = jnp.sum(squares, axis=1, keepdims=True)
    squares = row_of(wide(squares), diagonal(KEEP))
    pay = jnp.concatenate([mass, squares, jnp.zeros((6, HD), jnp.float32)], axis=0)
    pay_ref[...] = jnp.broadcast_to(pay[None], (TP, 8, HD))


def finish_kernel(pay_ref, rows_ref, gain_ref, text_ref, mass_ref, kept_ref):
    pay = jnp.sum(pay_ref[...], axis=0)
    mass_ref[...] = pay[0:1] * (1.0 - text_ref[...].astype(jnp.float32))
    squares = jnp.where(diagonal(KEEP), jnp.broadcast_to(pay[1:2], (KEEP, HD)), 0.0)
    factor = lax.rsqrt(wide(jnp.sum(squares, axis=1, keepdims=True)) / D + 1e-06)
    for h in range(GROUP):
        columns = slice(h * HD, (h + 1) * HD)
        rows = slice((h & 3) * KEEP, ((h & 3) + 1) * KEEP)
        side = slice((h >> 2) * HD, ((h >> 2) + 1) * HD)
        kept_ref[:, columns] = (rows_ref[rows, side] * factor * gain_ref[:, columns]).astype(
            jnp.bfloat16
        )


def shape_of(shape, dtype):
    return jax.ShapeDtypeStruct(shape, dtype)


def shifted(value, axis, step, count):
    return lax.ppermute(value, axis, [(i, (i + step) % count) for i in range(count)])


def cost(flops):
    return pl.CostEstimate(flops=flops, bytes_accessed=2**10, transcendentals=0)


def on_device(queries, key_rows, value_rows, text_mask, kept_slot, norm_gain):
    f32, bf16 = jnp.float32, jnp.bfloat16
    both = jnp.stack([key_rows, value_rows])
    over_z = ("zh", "zl")
    same = jnp.stack([both] + [shifted(both, over_z, step, NZ) for step in (4, 2, -2)])
    other = shifted(same, over_z, -1, NZ)
    state = [shape_of((ROWS, HD), f32)] * 3
    level = shape_of((GROUP, TOK), f32)
    near_weights = shape_of((ROWS, len(NEAR) * TOK), bf16)
    rest_weights = shape_of((ROWS, len(REST) * TOK), bf16)

    def kernel(body, name, inputs, out_shape, scratch=()):
        return pl.pallas_call(
            body,
            in_specs=[vmem()] * len(inputs),
            out_specs=[vmem()] * len(out_shape),
            out_shape=out_shape,
            scratch_shapes=list(scratch),
            compiler_params=params(),
            cost_estimate=cost(10**9),
            name=name,
        )(*inputs)

    *now, level_own, weights_own, pick_rows, pick_rest, slots, text = kernel(
        first_kernel,
        "first",
        [queries, same, kept_slot[None], text_mask[None]],
        state
        + [level, near_weights]
        + [shape_of((EIGHT, 4 * TOK), bf16), shape_of((EIGHT, 2 * TOK), bf16)]
        + [shape_of((TOK, HD), bf16), shape_of((8, TOK), f32)],
    )
    other, now[0] = lax.optimization_barrier((other, now[0]))
    left = [lax.ppermute(part, "x", TO_RIGHT) for part in (same, other)]
    right = [lax.ppermute(part, "x", TO_LEFT) for part in (same, other)]
    outs = kernel(
        second_kernel,
        "second",
        [queries, other, left[0], right[0], *now],
        state + [level] * 3 + [rest_weights, near_weights, near_weights],
    )
    now, levels, kept = list(outs[:3]), [level_own, *outs[3:6]], [weights_own, *outs[6:]]
    left[1], right[1], now[0] = lax.optimization_barrier((left[1], right[1], now[0]))
    half = 2
    far = []
    for i in range(2):
        far.append(lax.ppermute(left[i][:half], "x", FAR_RIGHT))
        far.append(lax.ppermute(right[i][half:], "x", FAR_LEFT))
    outs = kernel(
        third_kernel,
        "third",
        [queries, left[1], right[1], *far[:2], *now],
        state + [level] * 3 + [rest_weights, rest_weights, near_weights],
    )
    now, levels, kept = outs[:3], [*levels, *outs[3:6]], [*kept, *outs[6:]]
    context, send = kernel(
        last_kernel,
        "last",
        [queries, *far[2:], text, pick_rows, pick_rest, slots, *now, *levels, *kept],
        [shape_of((TOK, GROUP * HD), bf16), shape_of((SEND, HD), bf16)],
        [pltpu.VMEM((ROWS, HD), f32)] * 3
        + [pltpu.VMEM((ROWS, len(REST) * TOK), bf16), pltpu.VMEM((SHARDS, HD), f32)],
    )
    got = lax.all_to_all(
        send.reshape(SHARDS, SUB, HD), ("x", "zh", "zl"), split_axis=0, concat_axis=0, tiled=True
    ).reshape(SEND, HD)
    rows, pay = pl.pallas_call(
        place_kernel,
        in_specs=[vmem()],
        out_specs=[vmem()] * 2,
        out_shape=[shape_of((4 * KEEP, 2 * HD), f32), shape_of((TP, 8, HD), f32)],
        compiler_params=params(),
        name="place_rows",
    )(got)
    pay = lax.all_to_all(pay, ("y", "core"), split_axis=0, concat_axis=0, tiled=True)
    mass, kept = pl.pallas_call(
        finish_kernel,
        in_specs=[vmem()] * 4,
        out_specs=[vmem()] * 2,
        out_shape=[shape_of((1, TOK), f32), shape_of((KEEP, GROUP * HD), bf16)],
        compiler_params=params(),
        name="finish",
    )(pay, rows, norm_gain[None], text_mask[None])
    return context, mass[0], kept


def solution(mesh):
    cut = Mesh(mesh.devices.reshape(NX, NZ // 2, 2, 4, 2), ("x", "zh", "zl", "y", "core"))
    seq, tp = ("x", "zh", "zl"), ("y", "core")
    placed = (P(seq, tp), P(seq, tp), P(seq, tp), P(seq), P(seq), P(tp))
    return jax.shard_map(
        on_device,
        mesh=cut,
        in_specs=placed,
        out_specs=(P(seq, tp), P(seq), P(seq, tp)),
        check_vma=False,
    )
```

```python
import math

import jax
import jax.numpy as jnp
from jax import lax
from jax.experimental import pallas as pl
from jax.experimental.pallas import tpu as pltpu
from jax.sharding import Mesh, PartitionSpec as P

HD = 128
D = 8192
TOK = 128
GROUP = 8
ROWS = GROUP * TOK
NX = 4
NZ = 8
SHARDS = NX * NZ
KEEP = 32
SUB = 24
SEND = SHARDS * SUB
EIGHT = SHARDS * 8
TP = 8
NEAR = (0, 4, -2, 2)
REST = ((0,), (4,), (-2,), (2,))
FACTOR = math.log2(math.e) / math.sqrt(HD)
LOW = -1e30
NT = (((1,), (1,)), ((), ()))
TN = (((0,), (0,)), ((), ()))
VMEM_BYTES = 40 * 1024 * 1024


def vmem():
    return pl.BlockSpec(memory_space=pltpu.VMEM)


def params():
    return pltpu.CompilerParams(vmem_limit_bytes=VMEM_BYTES)


def wide(column):
    return jnp.broadcast_to(column, (column.shape[0], 128))


def tiled(array, count):
    return jnp.concatenate([array] * count, axis=1)


def position():
    return lax.axis_index("x"), lax.axis_index("zh") * 2 + lax.axis_index("zl")


def diagonal(rows=TOK):
    return lax.broadcasted_iota(jnp.int32, (rows, TOK), 0) == lax.broadcasted_iota(
        jnp.int32, (rows, TOK), 1
    )


def row_of(column, eye):
    return jnp.sum(jnp.where(eye, column, 0.0), axis=0, keepdims=True)


def rows_of(ref, eye):
    return jnp.concatenate(
        [row_of(ref[h * TOK : (h + 1) * TOK], eye) for h in range(GROUP)], axis=0
    )


def keys_of(*refs):
    return jnp.concatenate([ref[:, 0].reshape(-1, HD) for ref in refs], axis=0)


def values_of(*refs):
    value = jnp.concatenate([ref[:, 1].reshape(-1, HD) for ref in refs], axis=0)
    return jnp.concatenate([value, jnp.ones_like(value)], axis=1)


def shard_of(z, offset):
    if isinstance(offset, tuple):
        return shard_of(z ^ 1, offset[0])
    return (z + offset) & (NZ - 1)


def flash(query, key, value, old, weights_ref, rows, allowed=None):
    count = key.shape[0] // TOK
    scores = lax.dot_general(query, key, NT, preferred_element_type=jnp.float32)
    if allowed is not None:
        scores = jnp.where(allowed, scores, LOW)
    best = scores[:, 0:TOK]
    for i in range(1, count):
        best = jnp.maximum(best, scores[:, i * TOK : (i + 1) * TOK])
    top = wide(jnp.max(best, axis=1, keepdims=True))
    if old is not None:
        top = jnp.maximum(old[0], top)
    weights = jnp.exp2((scores - tiled(top, count)) * FACTOR).astype(jnp.bfloat16)
    weights_ref[rows] = weights
    both = jnp.dot(weights, value, preferred_element_type=jnp.float32)
    mixed, total = both[:, :HD], both[:, HD:]
    if old is not None:
        shrink = jnp.exp2((old[0] - top) * FACTOR)
        total = total + old[1] * shrink
        mixed = mixed + old[2] * shrink
    return top, total, mixed


def flash_heads(q_ref, pair, old_state, state, weights_ref, allowed=None):
    key = keys_of(*pair)
    value = values_of(*pair)
    for h in range(GROUP):
        rows = slice(h * TOK, (h + 1) * TOK)
        query = q_ref[:, h * HD : (h + 1) * HD]
        old = None if old_state is None else tuple(ref[rows] for ref in old_state)
        for ref, part in zip(state, flash(query, key, value, old, weights_ref, rows, allowed)):
            ref[rows] = part


def copy_state(old_state, state):
    for ref, old in zip(state, old_state):
        ref[...] = old[...]


def own_part(offsets, q_ref, keys_ref, old_state, state, level_ref, weights_ref):
    z = position()[1]
    token = lax.broadcasted_iota(jnp.int32, (TOK, TOK), 0)
    lane = lax.broadcasted_iota(jnp.int32, (TOK, TOK), 1)
    allowed = jnp.concatenate(
        [lane - token <= (z - shard_of(z, offset)) * TOK for offset in offsets], axis=1
    )
    flash_heads(q_ref, (keys_ref,), old_state, state, weights_ref, allowed)
    level_ref[...] = rows_of(state[0], diagonal())


def sides(q_ref, left_ref, right_ref, state, level_refs, weights_refs):
    x = position()[0]
    eye = diagonal()

    @pl.when(x > 0)
    def _():
        flash_heads(q_ref, (left_ref,), state, state, weights_refs[0])

    level_refs[0][...] = rows_of(state[0], eye)

    @pl.when(x == NX - 1)
    def _():
        flash_heads(q_ref, (right_ref,), state, state, weights_refs[1])

    level_refs[1][...] = rows_of(state[0], eye)


def first_kernel(q_ref, keys_ref, slot_row_ref, text_ref, *refs):
    state, (level_ref, weights_ref), picked, text_out_ref = refs[:3], refs[3:5], refs[5:8], refs[8]
    text_out_ref[...] = jnp.broadcast_to(text_ref[...].astype(jnp.float32), (8, TOK))
    own_part(NEAR, q_ref, keys_ref, None, state, level_ref, weights_ref)
    pick(slot_row_ref, *picked)


def second_kernel(q_ref, keys_ref, left_ref, right_ref, *refs):
    old_state, state, levels, weights = refs[:3], refs[3:6], refs[6:9], refs[9:]
    own_part(REST, q_ref, keys_ref, old_state, state, levels[0], weights[0])
    sides(q_ref, left_ref, right_ref, state, levels[1:], weights[1:])


def third_kernel(q_ref, left_ref, right_ref, far_0_ref, far_1_ref, *refs):
    old_state, state, levels, weights = refs[:3], refs[3:6], refs[6:9], refs[9:]
    copy_state(old_state, state)
    sides(q_ref, left_ref, right_ref, state, levels, weights)

    @pl.when(position()[0] >= 2)
    def _():
        flash_heads(q_ref, (far_0_ref, far_1_ref), state, state, weights[2])

    levels[2][...] = rows_of(state[0], diagonal())


def pick(slot_row_ref, rows_ref, rest_ref, slots_ref):
    slot_row = slot_row_ref[...]
    slot_col = jnp.transpose(jnp.broadcast_to(slot_row, (TOK, TOK)))
    slots = jnp.where(slot_col >= 0, (slot_col & (KEEP - 1)) + 1, 0)
    slots_ref[...] = slots.astype(jnp.float32).astype(jnp.bfloat16)
    target_row = jnp.where(slot_row >= 0, slot_row >> 5, -1)
    target_col = jnp.where(slot_col >= 0, slot_col >> 5, -1)
    first = lax.broadcasted_iota(jnp.int32, (TOK, TOK), 0)
    second = lax.broadcasted_iota(jnp.int32, (TOK, TOK), 1)
    earlier = jnp.where((target_col == target_row) & (first < second), 1, 0)
    rank = jnp.sum(earlier, axis=0, keepdims=True)
    placed = jnp.where(target_row >= 0, target_row * 2 + rank, -1)[None]
    shape = (SHARDS, 8, TOK)
    to = lax.broadcasted_iota(jnp.int32, shape, 0)
    sub = lax.broadcasted_iota(jnp.int32, shape, 1)
    lane = lax.broadcasted_iota(jnp.int32, shape, 2)

    def one_hot(hit):
        return jnp.where(hit, 1.0, 0.0).reshape(EIGHT, TOK).astype(jnp.bfloat16)

    same = placed == to * 2 + (sub >> 2)
    for h in range(4):
        rows_ref[:, h * TOK : (h + 1) * TOK] = one_hot(same & ((sub & 3) == h))
    rest_ref[:, :TOK] = one_hot((placed == to * 2 + (sub - 2)) & ((sub == 2) | (sub == 3)))
    rest_ref[:, TOK:] = one_hot(lane == jnp.where(sub == 0, to, jnp.where(sub == 1, to + SHARDS, -1)))


def last_kernel(
    q_ref,
    far_2_ref,
    far_3_ref,
    text_ref,
    pick_rows_ref,
    pick_rest_ref,
    slots_ref,
    top_in,
    total_in,
    mixed_in,
    *refs,
):
    levels, weights = refs[:7], refs[7:14]
    context_ref, send_ref, top_ref, total_ref, mixed_ref, weights_last_ref, mass_ref = refs[14:]
    x, z = position()
    old_state = (top_in, total_in, mixed_in)
    state = (top_ref, total_ref, mixed_ref)
    mass_ref[...] = jnp.zeros_like(mass_ref)

    @pl.when(x >= 2)
    def _():
        flash_heads(q_ref, (far_2_ref, far_3_ref), old_state, state, weights_last_ref)

    @pl.when(x < 2)
    def _():
        copy_state(old_state, state)

    context = (mixed_ref[...] / total_ref[...]).astype(jnp.bfloat16)
    for h in range(GROUP):
        context_ref[:, h * HD : (h + 1) * HD] = context[h * TOK : (h + 1) * TOK]

    text = text_ref[...]

    @pl.when(jnp.max(text) > 0.0)
    def _():
        eye = diagonal()
        level = rows_of(top_ref, eye)
        part = text / rows_of(total_ref, eye)

        def mass_of(level_then, weights_ref, at, offsets=NEAR):
            share = jnp.exp2((level_then - level) * FACTOR) * part
            share = jnp.concatenate([share[h : h + 1] for h in range(GROUP)], axis=1)
            high = share.astype(jnp.bfloat16).astype(jnp.float32)
            low = share - high
            both = jnp.concatenate(
                [jnp.broadcast_to(high, (8, ROWS)), jnp.broadcast_to(low, (8, ROWS))], axis=0
            ).astype(jnp.bfloat16)
            added = jnp.dot(both, weights_ref[...], preferred_element_type=jnp.float32)
            added = added[0:1] + added[8:9]
            shift = lax.rem(at, NX) * NZ
            for i, offset in enumerate(offsets):
                to = shift + shard_of(z, offset)
                mass_ref[pl.ds(to, 1), :] = added[:, i * TOK : (i + 1) * TOK]

        own, own_other, left, right, left_other, right_other, far = [
            (level_ref[...], weights_ref) for level_ref, weights_ref in zip(levels, weights)
        ]
        mass_of(*own, x)
        mass_of(*own_other, x, REST)

        @pl.when(x > 0)
        def _():
            mass_of(*left, x + NX - 1)
            mass_of(*left_other, x + NX - 1, REST)

        @pl.when(x == NX - 1)
        def _():
            mass_of(*right, x + 1)
            mass_of(*right_other, x + 1, REST)

        @pl.when(x >= 2)
        def _():
            mass_of(*far, x + 2)
            mass_of(level, weights_last_ref, x + 2, REST)

    half = ROWS // 2
    sides = jnp.concatenate([context[:half], context[half:]], axis=1)
    sides = jnp.dot(pick_rows_ref[...], sides, preferred_element_type=jnp.float32)
    mass = mass_ref[...]
    high = mass.astype(jnp.bfloat16).astype(jnp.float32)
    low = mass - high
    rest = jnp.concatenate([high, low, jnp.zeros((TOK - 2 * SHARDS, HD), jnp.float32)], axis=0)
    rest = jnp.concatenate([slots_ref[...], rest.astype(jnp.bfloat16)], axis=0)
    rest = jnp.dot(pick_rest_ref[...], rest, preferred_element_type=jnp.float32)
    parts = [part.reshape(SHARDS, 8, HD) for part in (sides[:, :HD], sides[:, HD:], rest)]
    send = jnp.concatenate(parts, axis=1).reshape(SEND, HD)
    send_ref[...] = send.astype(jnp.bfloat16)


def place_kernel(got_ref, rows_ref, pay_ref):
    got = got_ref[...].astype(jnp.float32).reshape(SHARDS, SUB, HD)
    mass = jnp.sum(got[:, 16:17, :] + got[:, 17:18, :], axis=0)
    slots = jnp.concatenate(
        [
            jnp.broadcast_to(got[:, 18:19, :], (SHARDS, 4, HD)),
            jnp.broadcast_to(got[:, 19:20, :], (SHARDS, 4, HD)),
        ],
        axis=1,
    ).astype(jnp.int32)
    shape = (SHARDS, 8, HD)
    head = lax.broadcasted_iota(jnp.int32, shape, 1) & 3
    lane = lax.broadcasted_iota(jnp.int32, shape, 2)
    hit = (slots == (lane & (KEEP - 1)) + 1) & (head == lane >> 5)
    put = jnp.where(hit, 1.0, 0.0).reshape(EIGHT, HD).astype(jnp.bfloat16)
    sides = jnp.concatenate(
        [got[:, 0:8].reshape(EIGHT, HD), got[:, 8:16].reshape(EIGHT, HD)], axis=1
    ).astype(jnp.bfloat16)
    rows = lax.dot_general(put, sides, TN, preferred_element_type=jnp.float32)
    rows_ref[...] = rows
    squares = jnp.sum((rows * rows).reshape(4, KEEP, 2 * HD), axis=0)
    squares = jnp.sum(squares, axis=1, keepdims=True)
    squares = row_of(wide(squares), diagonal(KEEP))
    pay = jnp.concatenate([mass, squares, jnp.zeros((6, HD), jnp.float32)], axis=0)
    pay_ref[...] = jnp.broadcast_to(pay[None], (TP, 8, HD))


def finish_kernel(pay_ref, rows_ref, gain_ref, text_ref, mass_ref, kept_ref):
    pay = jnp.sum(pay_ref[...], axis=0)
    mass_ref[...] = pay[0:1] * (1.0 - text_ref[...].astype(jnp.float32))
    squares = jnp.where(diagonal(KEEP), jnp.broadcast_to(pay[1:2], (KEEP, HD)), 0.0)
    factor = lax.rsqrt(wide(jnp.sum(squares, axis=1, keepdims=True)) / D + 1e-06)
    for h in range(GROUP):
        columns = slice(h * HD, (h + 1) * HD)
        rows = slice((h & 3) * KEEP, ((h & 3) + 1) * KEEP)
        side = slice((h >> 2) * HD, ((h >> 2) + 1) * HD)
        kept_ref[:, columns] = (rows_ref[rows, side] * factor * gain_ref[:, columns]).astype(
            jnp.bfloat16
        )


def shape_of(shape, dtype):
    return jax.ShapeDtypeStruct(shape, dtype)


def shifted(value, axis, step, count):
    return lax.ppermute(value, axis, [(i, (i + step) % count) for i in range(count)])


def cost(flops):
    return pl.CostEstimate(flops=flops, bytes_accessed=2**10, transcendentals=0)


def on_device(queries, key_rows, value_rows, text_mask, kept_slot, norm_gain):
    f32, bf16 = jnp.float32, jnp.bfloat16
    both = jnp.stack([key_rows, value_rows])
    over_z = ("zh", "zl")
    same = jnp.stack([both] + [shifted(both, over_z, step, NZ) for step in (4, 2, -2)])
    other = shifted(same, "zl", 1, 2)
    state = [shape_of((ROWS, HD), f32)] * 3
    level = shape_of((GROUP, TOK), f32)
    near_weights = shape_of((ROWS, len(NEAR) * TOK), bf16)
    rest_weights = shape_of((ROWS, len(REST) * TOK), bf16)

    def kernel(body, name, inputs, out_shape, scratch=()):
        return pl.pallas_call(
            body,
            in_specs=[vmem()] * len(inputs),
            out_specs=[vmem()] * len(out_shape),
            out_shape=out_shape,
            scratch_shapes=list(scratch),
            compiler_params=params(),
            cost_estimate=cost(10**9),
            name=name,
        )(*inputs)

    *now, level_own, weights_own, pick_rows, pick_rest, slots, text = kernel(
        first_kernel,
        "first",
        [queries, same, kept_slot[None], text_mask[None]],
        state
        + [level, near_weights]
        + [shape_of((EIGHT, 4 * TOK), bf16), shape_of((EIGHT, 2 * TOK), bf16)]
        + [shape_of((TOK, HD), bf16), shape_of((8, TOK), f32)],
    )
    other, now[0] = lax.optimization_barrier((other, now[0]))
    left = [shifted(part, "x", 1, NX) for part in (same, other)]
    right = [shifted(part, "x", -1, NX) for part in (same, other)]
    outs = kernel(
        second_kernel,
        "second",
        [queries, other, left[0], right[0], *now],
        state + [level] * 3 + [rest_weights, near_weights, near_weights],
    )
    now, levels, kept = list(outs[:3]), [level_own, *outs[3:6]], [weights_own, *outs[6:]]
    left[1], right[1], now[0] = lax.optimization_barrier((left[1], right[1], now[0]))
    half = 2
    far = []
    for i in range(2):
        far.append(shifted(left[i][:half], "x", 1, NX))
        far.append(shifted(right[i][half:], "x", -1, NX))
    outs = kernel(
        third_kernel,
        "third",
        [queries, left[1], right[1], *far[:2], *now],
        state + [level] * 3 + [rest_weights, rest_weights, near_weights],
    )
    now, levels, kept = outs[:3], [*levels, *outs[3:6]], [*kept, *outs[6:]]
    context, send = kernel(
        last_kernel,
        "last",
        [queries, *far[2:], text, pick_rows, pick_rest, slots, *now, *levels, *kept],
        [shape_of((TOK, GROUP * HD), bf16), shape_of((SEND, HD), bf16)],
        [pltpu.VMEM((ROWS, HD), f32)] * 3
        + [pltpu.VMEM((ROWS, len(REST) * TOK), bf16), pltpu.VMEM((SHARDS, HD), f32)],
    )
    got = lax.all_to_all(
        send.reshape(SHARDS, SUB, HD), ("x", "zh", "zl"), split_axis=0, concat_axis=0, tiled=True
    ).reshape(SEND, HD)
    rows, pay = pl.pallas_call(
        place_kernel,
        in_specs=[vmem()],
        out_specs=[vmem()] * 2,
        out_shape=[shape_of((4 * KEEP, 2 * HD), f32), shape_of((TP, 8, HD), f32)],
        compiler_params=params(),
        name="place_rows",
    )(got)
    pay = lax.all_to_all(pay, ("y", "core"), split_axis=0, concat_axis=0, tiled=True)
    mass, kept = pl.pallas_call(
        finish_kernel,
        in_specs=[vmem()] * 4,
        out_specs=[vmem()] * 2,
        out_shape=[shape_of((1, TOK), f32), shape_of((KEEP, GROUP * HD), bf16)],
        compiler_params=params(),
        name="finish",
    )(pay, rows, norm_gain[None], text_mask[None])
    return context, mass[0], kept


def solution(mesh):
    cut = Mesh(mesh.devices.reshape(NX, NZ // 2, 2, 4, 2), ("x", "zh", "zl", "y", "core"))
    seq, tp = ("x", "zh", "zl"), ("y", "core")
    placed = (P(seq, tp), P(seq, tp), P(seq, tp), P(seq), P(seq), P(tp))
    return jax.shard_map(
        on_device,
        mesh=cut,
        in_specs=placed,
        out_specs=(P(seq, tp), P(seq), P(seq, tp)),
        check_vma=False,
    )
```
